32 devices in a mesh: ctx: 8 (over z, core), exp: 4 (over y, x).
Axes of the slice: x: 2, y: 2, z: 4, core: 2. Of those that a mesh axis runs over, the one named last changes fastest.
Arguments:
- grad_out: bfloat16 [4, 1024, 4096], P('exp', 'ctx'), may hold values from -1.796875 to 1.796875
- routes: int32 [4, 1024, 1], P('exp', 'ctx'), may hold values from 0 to 3; in each aligned block of 128 rows (0 to 127, 128 to 255, ..., all dimensions but the last counted through in order) at most 48 rows name the same one
- gate_probs: float32 [4, 1024, 1], P('exp', 'ctx'), may hold values from 0.2 to 1
- saved_pre: bfloat16 [8, 4, 192, 1536], P('ctx', 'exp'), may hold values from -6 to 6
- down_weight: bfloat16 [4, 768, 4096], P('exp', None, 'ctx'), may hold values from -0.21875 to 0.21875
- gate_up_weight: bfloat16 [4, 4096, 1536], P('exp', 'ctx'), may hold values from -0.21875 to 0.21875
- queries: bfloat16 [4, 1024, 4096], P('exp', 'ctx')
- keys_values: bfloat16 [4, 1024, 512], P('exp', 'ctx')
- attn_grad: bfloat16 [4, 1024, 4096], P('exp', 'ctx'), may hold values from -6 to 6
- attn_out: bfloat16 [4, 1024, 4096], P('exp', 'ctx'), may hold values from -6 to 6
Outputs:
- moe_input_grad: bfloat16 [4, 1024, 4096], P('exp', 'ctx')
- prob_grad: bfloat16 [4, 1024, 1], P('exp', 'ctx')
- query_grad: bfloat16 [4, 1024, 4096], P('exp', 'ctx')
- kv_grad: bfloat16 [4, 1024, 512], P('exp', 'ctx')
The draws below stay inside these ranges and needn't reach their ends.
Inputs may be any that keep to these rules, and one draw needn't show every extreme that they name: `routes`: in the rows of one device no expert is named by more than 48 tokens, a bound that some block reaches.
All inputs are finite; a program needn't handle non-finite values.
Results may differ from the reference program's by a relative error of at most 0.0065.
Values may be sent and summed in bfloat16 or wider, within the bound.
A program may use at most 192 MiB of HBM per device.

```python
import math
import jax
import jax.numpy as jnp
import numpy as np
from jax import lax

D = 4096
FFW = 768
QUERY_HEAD_COUNT = 32
KEY_VALUE_HEADS = 2
HEAD_SIZE = 128
TOPK = 1
TOK_DEV = 128
EXPERTS = 4
SEQUENCE_COUNT = 4
SEQUENCE_LENGTH = 1024
CAP = 48
N_CTX = 8
N_EXP = 4


def shared_keys(key):
    starting_keys = jax.random.normal(key, (SEQUENCE_COUNT, SEQUENCE_LENGTH, KEY_VALUE_HEADS, HEAD_SIZE), jnp.float32)
    anchor = jnp.arange(40, SEQUENCE_LENGTH, 53)
    blended = starting_keys[:, anchor - 17]
    return starting_keys.at[:, anchor - 17].set(blended)


def draw_keys_values(key, part):
    key_rows = shared_keys(key)
    key = jax.random.fold_in(key, 7)
    value_tensor = jax.random.normal(key, (SEQUENCE_COUNT, SEQUENCE_LENGTH, KEY_VALUE_HEADS, HEAD_SIZE), jnp.float32)
    joined_parts = jnp.concatenate([key_rows, value_tensor], axis=-1)
    return joined_parts.reshape(SEQUENCE_COUNT, SEQUENCE_LENGTH, KEY_VALUE_HEADS * 2 * HEAD_SIZE).astype(jnp.bfloat16)


def draw_queries(key, part):
    key = jax.random.fold_in(key, 5)
    queries = jax.random.normal(key, (SEQUENCE_COUNT, SEQUENCE_LENGTH, QUERY_HEAD_COUNT, HEAD_SIZE), jnp.float32)
    return queries.reshape(SEQUENCE_COUNT, SEQUENCE_LENGTH, QUERY_HEAD_COUNT * HEAD_SIZE).astype(jnp.bfloat16)


def level_of(stream_key, dims, shards, smallest, high):
    factor_of, own = 1.0, jax.random.fold_in(stream_key, 6)
    for dim, parts in shards:
        steps = jnp.exp(jax.random.uniform(jax.random.fold_in(own, dim), (parts,), jnp.float32, smallest / len(shards), high / len(shards)))
        factor_of = factor_of * jnp.repeat(steps, dims[dim] // parts).reshape([-1 if axis == dim else 1 for axis in range(len(dims))])
    return factor_of


def assign_block(stream_key, own, number, rows, count, top, most, lean):
    sequence = jax.random.permutation(stream_key, count)
    heavy_load, common = shares(count, rows * top, most, lean, True), shares(count, rows * top, most, lean, False)
    places = jnp.arange(count)

    def named(tallies, offset_by):
        used = int((tallies > 0).sum())
        fixed = max(1, used // 4)
        shifted = fixed + (places - fixed + offset_by * (used - fixed)) % max(1, count - fixed)
        return jnp.zeros((count,), jnp.int32).at[sequence[jnp.where(places < fixed, places, shifted)]].set(jnp.asarray(tallies, jnp.int32))

    tallies = jnp.where(number % 4 == 0, named(heavy_load, number // 4), named(common, number - number // 4 - 1))
    mixed = jax.random.permutation(jax.random.fold_in(own, 3), count)
    donor, receiver = mixed[0:count // 2 * 2:2], mixed[1:count // 2 * 2:2]
    slack = jnp.minimum(tallies[donor] - 1, most - tallies[receiver]) // 2
    slack = jnp.where((donor == sequence[0]) | (receiver == sequence[0]) | (tallies[receiver] == 0), 0, jnp.maximum(slack, 0))
    shifted = jax.random.randint(jax.random.fold_in(own, 4), (count // 2,), 0, 1 << 20) % (slack + 1)
    tallies = tallies.at[donor].add(-shifted).at[receiver].add(shifted)
    members = jnp.searchsorted(jnp.cumsum(tallies), jnp.arange(rows * top), side="right").astype(jnp.int32)
    listing = members.reshape(top, rows).T
    listing = listing[jax.random.permutation(jax.random.fold_in(own, 1), rows)]
    offset_by = jax.random.randint(jax.random.fold_in(own, 2), (rows, 1), 0, top)
    return jnp.take_along_axis(listing, (jnp.arange(top)[None, :] + offset_by) % top, axis=1)


def shares(count, total, bound, lean, full):
    weights = [(1 << 20) // math.isqrt(rank ** lean) + 1 for rank in range(1, count + 1)]
    largest = bound if full else min(bound, max(-(-total // count), total * weights[0] // sum(weights)))
    least = 1 if total - largest >= count - 1 else 0
    counts, spare = [largest] + [least] * (count - 1), total - largest - least * (count - 1)
    while spare > 0:
        movable = [i for i in range(1, count) if counts[i] < largest] or [i for i in range(1, count) if counts[i] < bound]
        pool, budget = sum([weights[i] for i in movable]), spare
        for i in movable:
            addition = min(bound - counts[i], max(1, budget * weights[i] // pool), spare)
            counts[i] = counts[i] + addition
            spare = spare - addition
    return np.array(counts)


def centred(stream_key, shape, spread, bound, split=(), held_as=jnp.bfloat16):
    values = jax.random.normal(stream_key, shape, jnp.float32) * spread
    if len(split) > 0:
        values = level_of(stream_key, shape, split, -0.22, 0.18) * values
    return jnp.clip(values, min=-bound, max=bound).astype(held_as)


def setup_inputs(seed: int = 0) -> dict:
    keys = jax.random.split(jax.random.key(seed), 11)
    grad_out = centred(keys[0], (SEQUENCE_COUNT, SEQUENCE_LENGTH, D), 0.3, 1.796875, ((0, 4), (1, 8)))
    routes_keys = jax.random.split(jax.random.fold_in(keys[1], 1), SEQUENCE_COUNT * SEQUENCE_LENGTH // TOK_DEV)
    routes_turns = jax.random.permutation(jax.random.fold_in(keys[1], 3), SEQUENCE_COUNT * SEQUENCE_LENGTH // TOK_DEV)
    routes = jax.vmap(lambda own, number: assign_block(jax.random.fold_in(keys[1], 2), own, number, TOK_DEV, EXPERTS, TOPK, CAP, 2))(routes_keys, routes_turns).reshape((SEQUENCE_COUNT, SEQUENCE_LENGTH, TOPK))
    gate_probs = jnp.clip(0.2 + 0.8 * jax.random.uniform(keys[2], (SEQUENCE_COUNT, SEQUENCE_LENGTH, TOPK), jnp.float32) ** level_of(keys[2], (SEQUENCE_COUNT, SEQUENCE_LENGTH, TOPK), ((0, 4), (1, 8)), -0.2, 0.2), 0.2, 1.0)
    saved_pre = centred(keys[3], (N_CTX, EXPERTS, N_EXP * CAP, 2 * FFW), 1.0, 6.0, ((0, 8), (1, 4)))
    down_weight = centred(keys[4], (EXPERTS, FFW, D), FFW ** -0.5, 0.21875, ((0, 4), (2, 8)))
    gate_up_weight = centred(keys[5], (EXPERTS, D, 2 * FFW), FFW ** -0.5, 0.21875, ((0, 4), (1, 8)))
    queries = draw_queries(jax.random.fold_in(keys[10], 71), 0)
    keys_values = draw_keys_values(jax.random.fold_in(keys[10], 71), 0)
    attn_grad = centred(keys[8], (SEQUENCE_COUNT, SEQUENCE_LENGTH, QUERY_HEAD_COUNT * HEAD_SIZE), 1.0, 6.0, ((0, 4), (1, 8)))
    attn_out = centred(keys[9], (SEQUENCE_COUNT, SEQUENCE_LENGTH, QUERY_HEAD_COUNT * HEAD_SIZE), 1.0, 6.0, ((0, 4), (1, 8)))
    return {"grad_out": grad_out, "routes": routes, "gate_probs": gate_probs, "saved_pre": saved_pre, "down_weight": down_weight, "gate_up_weight": gate_up_weight, "queries": queries, "keys_values": keys_values, "attn_grad": attn_grad, "attn_out": attn_out}


def slot_table(route_grid):
    flat_routes = route_grid.reshape(N_EXP, N_CTX, TOK_DEV * TOPK)
    one_hot = (flat_routes[..., None] == jnp.arange(EXPERTS, dtype=jnp.int32)).astype(jnp.int32)
    earlier = jnp.cumsum(one_hot, axis=2) - one_hot
    positions = jnp.sum(earlier * one_hot, axis=-1)
    return positions.reshape(N_EXP, N_CTX, TOK_DEV, TOPK).astype(jnp.int32)


def expert_backward(expert_rows, pre_acts, down_block, gate_up_block):
    down_grad = jnp.dot(expert_rows, down_block.T, preferred_element_type=jnp.float32)
    gate_pre = pre_acts[:, :FFW].astype(jnp.float32)
    up_pre = pre_acts[:, FFW:].astype(jnp.float32)
    sigma = jax.nn.sigmoid(gate_pre)
    swish = gate_pre * sigma
    slot_prob = jnp.sum(down_grad * swish * up_pre, axis=-1).astype(jnp.bfloat16)
    gate_part = down_grad * up_pre * sigma * (1.0 + gate_pre * (1.0 - sigma))
    up_part = down_grad * swish
    pre_grad = jnp.concatenate([gate_part, up_part], axis=-1).astype(jnp.bfloat16)
    slot_input = jnp.dot(pre_grad, gate_up_block.T, preferred_element_type=jnp.float32).astype(jnp.bfloat16)
    return slot_input, slot_prob


def moe_backward(grad_out, routes, gate_probs, saved_pre, down_weight, gate_up_weight):
    route_grid = routes.reshape(N_EXP, N_CTX, TOK_DEV, TOPK)
    prob_grid = gate_probs.reshape(N_EXP, N_CTX, TOK_DEV, TOPK)
    grad_grid = grad_out.reshape(N_EXP, N_CTX, TOK_DEV, D)
    positions = slot_table(route_grid)
    padded = jnp.concatenate([grad_grid, jnp.zeros((N_EXP, N_CTX, 1, D), grad_grid.dtype)], axis=2)
    shape_four = (N_EXP, N_CTX, TOK_DEV, TOPK)
    source_ids = jnp.broadcast_to(jnp.arange(N_EXP, dtype=jnp.int32)[:, None, None, None], shape_four)
    block_ids = jnp.broadcast_to(jnp.arange(N_CTX, dtype=jnp.int32)[None, :, None, None], shape_four)
    token_ids = jnp.broadcast_to(jnp.arange(TOK_DEV, dtype=jnp.int32)[None, None, :, None], shape_four)
    table = jnp.full((N_EXP, N_CTX, EXPERTS, CAP), TOK_DEV, jnp.int32)
    table = table.at[source_ids, block_ids, route_grid, positions].set(token_ids)

    def per_expert(carry, expert):
        input_acc, prob_acc = carry
        lookup = table[:, :, expert, :]
        gathered = jnp.take_along_axis(padded, lookup[..., None], axis=2)
        expert_rows = jnp.transpose(gathered, (1, 0, 2, 3)).reshape(N_CTX * N_EXP * CAP, D)
        pre_acts = saved_pre[:, expert].reshape(N_CTX * N_EXP * CAP, 2 * FFW)
        slot_input, slot_prob = expert_backward(expert_rows, pre_acts, down_weight[expert], gate_up_weight[expert])
        input_grid = jnp.transpose(slot_input.reshape(N_CTX, N_EXP, CAP, D), (1, 0, 2, 3))
        slot_grid = jnp.transpose(slot_prob.reshape(N_CTX, N_EXP, CAP), (1, 0, 2))
        for which in range(TOPK):
            chosen = route_grid[..., which] == expert
            slot_here = positions[..., which]
            picked = jnp.take_along_axis(input_grid, slot_here[..., None], axis=2)
            weight_here = jnp.where(chosen, prob_grid[..., which], jnp.float32(0.0))
            input_acc = input_acc + weight_here[..., None] * picked.astype(jnp.float32)
            prob_pick = jnp.take_along_axis(slot_grid, slot_here, axis=2).astype(jnp.float32)
            prob_acc = prob_acc.at[..., which].add(jnp.where(chosen, prob_pick, jnp.float32(0.0)))
        return (input_acc, prob_acc), None

    start_carry = (jnp.zeros((N_EXP, N_CTX, TOK_DEV, D), jnp.float32),
                   jnp.zeros((N_EXP, N_CTX, TOK_DEV, TOPK), jnp.float32))
    (input_acc, prob_acc), unused = lax.scan(per_expert, start_carry, jnp.arange(EXPERTS, dtype=jnp.int32))
    moe_input_grad = input_acc.astype(jnp.bfloat16).reshape(SEQUENCE_COUNT, SEQUENCE_LENGTH, D)
    prob_grad = prob_acc.astype(jnp.bfloat16).reshape(SEQUENCE_COUNT, SEQUENCE_LENGTH, TOPK)
    return moe_input_grad, prob_grad


def head_backward(items):
    query, grad_head, out_head, key_rows, value_rows = items
    scale = HEAD_SIZE ** -0.5
    scores = jnp.dot(query, key_rows.T, preferred_element_type=jnp.float32) * scale
    causal = jnp.arange(SEQUENCE_LENGTH)[:, None] >= jnp.arange(SEQUENCE_LENGTH)[None, :]
    scores = jnp.where(causal, scores, jnp.float32(-1e30))
    highest = jnp.max(scores, axis=-1, keepdims=True)
    expo = jnp.exp(scores - highest)
    probs = expo / jnp.sum(expo, axis=-1, keepdims=True)
    low_probs = probs.astype(jnp.bfloat16)
    value_grad = jnp.dot(low_probs.T, grad_head, preferred_element_type=jnp.float32)
    prob_part = jnp.dot(grad_head, value_rows.T, preferred_element_type=jnp.float32)
    delta = jnp.sum(grad_head.astype(jnp.float32) * out_head.astype(jnp.float32), axis=-1, keepdims=True)
    score_grad = (probs * (prob_part - delta)).astype(jnp.bfloat16)
    query_part = jnp.dot(score_grad, key_rows, preferred_element_type=jnp.float32) * scale
    key_portion = jnp.dot(score_grad.T, query, preferred_element_type=jnp.float32) * scale
    return query_part, key_portion, value_grad


def sequence_backward(items):
    query_seq, grad_seq, out_seq, key_value_sequence = items
    query_group = QUERY_HEAD_COUNT // KEY_VALUE_HEADS
    query_heads = jnp.transpose(query_seq.reshape(SEQUENCE_LENGTH, QUERY_HEAD_COUNT, HEAD_SIZE), (1, 0, 2))
    grad_heads = jnp.transpose(grad_seq.reshape(SEQUENCE_LENGTH, QUERY_HEAD_COUNT, HEAD_SIZE), (1, 0, 2))
    out_heads = jnp.transpose(out_seq.reshape(SEQUENCE_LENGTH, QUERY_HEAD_COUNT, HEAD_SIZE), (1, 0, 2))
    key_value_heads = jnp.transpose(key_value_sequence.reshape(SEQUENCE_LENGTH, KEY_VALUE_HEADS, 2 * HEAD_SIZE), (1, 0, 2))
    owning_head = jnp.arange(QUERY_HEAD_COUNT, dtype=jnp.int32) // query_group
    key_heads = key_value_heads[owning_head][:, :, :HEAD_SIZE]
    value_heads = key_value_heads[owning_head][:, :, HEAD_SIZE:]
    query_part, key_portion, value_portion = lax.map(head_backward, (query_heads, grad_heads, out_heads, key_heads, value_heads))
    key_total_sum = jnp.sum(key_portion.reshape(KEY_VALUE_HEADS, query_group, SEQUENCE_LENGTH, HEAD_SIZE), axis=1)
    value_total_sum = jnp.sum(value_portion.reshape(KEY_VALUE_HEADS, query_group, SEQUENCE_LENGTH, HEAD_SIZE), axis=1)
    query_out = jnp.transpose(query_part, (1, 0, 2)).reshape(SEQUENCE_LENGTH, QUERY_HEAD_COUNT * HEAD_SIZE).astype(jnp.bfloat16)
    key_value_joined = jnp.concatenate([key_total_sum, value_total_sum], axis=-1)
    key_value_output = jnp.transpose(key_value_joined, (1, 0, 2)).reshape(SEQUENCE_LENGTH, KEY_VALUE_HEADS * 2 * HEAD_SIZE).astype(jnp.bfloat16)
    return query_out, key_value_output


def reference(grad_out, routes, gate_probs, saved_pre, down_weight, gate_up_weight, queries, keys_values, attn_grad, attn_out):
    moe_input_grad, prob_grad = moe_backward(grad_out, routes, gate_probs, saved_pre, down_weight, gate_up_weight)
    query_grad, kv_grad = lax.map(sequence_backward, (queries, attn_grad, attn_out, keys_values))
    return moe_input_grad, prob_grad, query_grad, kv_grad
```

```python
import functools

import jax
import jax.numpy as jnp
from jax import lax
from jax.experimental import pallas as pl
from jax.experimental.pallas import tpu as pltpu
from jax.sharding import PartitionSpec as P

KEY_VALUE_HEADS = 2
HEAD_SIZE = 128
LOG2E = 1.4426950408889634
NT = (((1,), (1,)), ((), ()))


def attention_kernel(
    pairs, pos_ref, q_ref, g_ref, o_ref, kv_ref, dq_ref, dkv_ref, kt_ref, bias_ref, st_ref, ds_ref
):
    seq_len = kv_ref.shape[0]
    rows = q_ref.shape[0]
    hd = HEAD_SIZE
    scale = hd**-0.5
    chunk = 256
    chunks = [pl.ds(i * chunk, chunk) for i in range(seq_len // chunk)]

    @pl.when(pl.program_id(1) == 0)
    def _():
        kt_ref[...] = kv_ref[:, :hd].astype(jnp.float32).T.astype(jnp.bfloat16)
        dkv_ref[...] = jnp.zeros_like(dkv_ref)
        key_pos = lax.broadcasted_iota(jnp.int32, bias_ref.shape, 0)
        row_pos = pos_ref[0] + lax.broadcasted_iota(jnp.int32, bias_ref.shape, 1) % rows
        bias_ref[...] = jnp.where(key_pos <= row_pos, 0.0, -1e30).astype(jnp.float32)

    for pair in range(pairs):
        cols = [pl.ds((2 * pair + i) * hd, hd) for i in range(2)]
        q2 = jnp.concatenate([q_ref[:, col] for col in cols], axis=0)
        g2 = jnp.concatenate([g_ref[:, col] for col in cols], axis=0)
        o2 = jnp.concatenate([o_ref[:, col] for col in cols], axis=0)
        prod = g2.astype(jnp.float32) * o2.astype(jnp.float32)
        delta = jnp.sum(prod.T, axis=0, keepdims=True)
        top = jnp.full((1, 2 * rows), -jnp.inf, jnp.float32)
        for part in chunks:
            s = lax.dot_general(kv_ref[part, :hd], q2, NT, preferred_element_type=jnp.float32)
            s = s + bias_ref[part, :]
            st_ref[pair, part, :] = s
            top = jnp.maximum(top, jnp.max(s, axis=0, keepdims=True))
        total = jnp.zeros((1, 2 * rows), jnp.float32)
        for part in chunks:
            e = jnp.exp2((st_ref[pair, part, :] - top) * (scale * LOG2E))
            st_ref[pair, part, :] = e
            total = total + jnp.sum(e, axis=0, keepdims=True)
        inverse = 1.0 / total
        for part in chunks:
            p = st_ref[pair, part, :] * inverse
            dkv_ref[part, hd:] += jnp.dot(
                p.astype(jnp.bfloat16), g2, preferred_element_type=jnp.float32
            )
            dp = lax.dot_general(kv_ref[part, hd:], g2, NT, preferred_element_type=jnp.float32)
            ds = (p * (dp - delta)).astype(jnp.bfloat16)
            ds_ref[pair, part, :] = ds
            dkv_ref[part, :hd] += jnp.dot(ds, q2, preferred_element_type=jnp.float32) * scale
        dqt = jnp.dot(kt_ref[...], ds_ref[pair], preferred_element_type=jnp.float32) * scale
        dq = dqt.T
        for i in range(2):
            dq_ref[:, cols[i]] = dq[i * rows : (i + 1) * rows].astype(dq_ref.dtype)


def attention(q, g, o, kv, first):
    rows, width = q.shape
    seq_len = kv.shape[0]
    hd = HEAD_SIZE
    pairs = 2
    step = pairs * 2 * hd
    steps = width // KEY_VALUE_HEADS // step
    tok = pl.BlockSpec((rows, step), lambda h, i: (0, h * steps + i))
    key = pl.BlockSpec((seq_len, 2 * hd), lambda h, i: (0, h))
    return pl.pallas_call(
        functools.partial(attention_kernel, pairs),
        grid=(KEY_VALUE_HEADS, steps),
        in_specs=[pl.BlockSpec(memory_space=pltpu.SMEM), tok, tok, tok, key],
        out_specs=[tok, key],
        out_shape=[
            jax.ShapeDtypeStruct((rows, width), jnp.bfloat16),
            jax.ShapeDtypeStruct((seq_len, kv.shape[1]), jnp.float32),
        ],
        scratch_shapes=[
            pltpu.VMEM((hd, seq_len), jnp.bfloat16),
            pltpu.VMEM((seq_len, 2 * rows), jnp.float32),
            pltpu.VMEM((pairs, seq_len, 2 * rows), jnp.float32),
            pltpu.VMEM((pairs, seq_len, 2 * rows), jnp.bfloat16),
        ],
        compiler_params=pltpu.CompilerParams(vmem_limit_bytes=40 * 1024 * 1024),
        cost_estimate=pl.CostEstimate(
            flops=10 * rows * seq_len * width,
            bytes_accessed=8 * rows * width + 6 * seq_len * kv.shape[1],
            transcendentals=rows * seq_len * width // hd,
        ),
    )(first, q, g, o, kv)


def body(
    grad_out,
    routes,
    gate_probs,
    saved_pre,
    down_weight,
    gate_up_weight,
    queries,
    keys_values,
    attn_grad,
    attn_out,
):
    experts = lax.axis_size("exp")
    contexts = lax.axis_size("ctx")
    tok_rows = grad_out.shape[1]
    width = grad_out.shape[2]
    capacity = saved_pre.shape[2] // experts
    hidden = down_weight.shape[1]
    chips = contexts // 2
    pair_groups = [[2 * i, 2 * i + 1] for i in range(chips)]
    chip_groups = [[2 * i + core for i in range(chips)] for core in range(2)]

    kv_all = lax.all_gather(keys_values[0], "ctx", axis=0, tiled=True)
    down_full = lax.all_gather(down_weight[0], "ctx", axis=1, tiled=True)
    gate_up = lax.all_gather(
        gate_up_weight[0], "ctx", axis=0, tiled=True, axis_index_groups=pair_groups
    )

    route_rows = routes[0]
    one_hot = (
        route_rows.reshape(-1)[:, None] == jnp.arange(experts, dtype=jnp.int32)[None, :]
    ).astype(jnp.int32)
    earlier = jnp.cumsum(one_hot, axis=0) - one_hot
    positions = jnp.sum(earlier * one_hot, axis=-1)
    slot_keys = route_rows[:, 0] * capacity + positions
    slots = experts * capacity
    dispatch = (jnp.arange(slots, dtype=jnp.int32)[:, None] == slot_keys[None, :]).astype(
        jnp.bfloat16
    )
    send_rows = jnp.dot(dispatch, grad_out[0], preferred_element_type=jnp.float32).astype(
        jnp.bfloat16
    )
    expert_rows = lax.all_to_all(
        send_rows.reshape(experts, capacity, width), "exp", split_axis=0, concat_axis=0, tiled=True
    ).reshape(slots, width)

    first = (lax.axis_index("ctx") * tok_rows).astype(jnp.int32).reshape(1)
    query_grad, kv_terms = attention(queries[0], attn_grad[0], attn_out[0], kv_all, first)
    kv_grad = lax.psum_scatter(kv_terms, "ctx", scatter_dimension=0, tiled=True).astype(
        jnp.bfloat16
    )

    down_grad = lax.dot_general(expert_rows, down_full, NT, preferred_element_type=jnp.float32)
    pre_acts = saved_pre[0, 0]
    gate_pre = pre_acts[:, :hidden].astype(jnp.float32)
    up_pre = pre_acts[:, hidden:].astype(jnp.float32)
    sigma = jax.nn.sigmoid(gate_pre)
    swish = gate_pre * sigma
    slot_prob = jnp.sum(down_grad * swish * up_pre, axis=-1).astype(jnp.bfloat16)
    gate_part = down_grad * up_pre * sigma * (1.0 + gate_pre * (1.0 - sigma))
    up_part = down_grad * swish
    pre_grad = jnp.concatenate([gate_part, up_part], axis=-1).astype(jnp.bfloat16)

    pre_all = lax.all_gather(pre_grad, "ctx", axis=0, tiled=True, axis_index_groups=chip_groups)
    slot_input = lax.dot_general(pre_all, gate_up, NT, preferred_element_type=jnp.float32).astype(
        jnp.bfloat16
    )
    columns = slot_input.shape[1]
    back = lax.all_to_all(
        slot_input.reshape(chips, experts, capacity, columns),
        "exp",
        split_axis=1,
        concat_axis=1,
        tiled=True,
    ).reshape(chips, slots, columns)
    keys_all, gates_all = (
        lax.all_gather(item, "ctx", axis=0, axis_index_groups=chip_groups)
        for item in (slot_keys, gate_probs[0, :, 0])
    )
    pick = (keys_all[:, :, None] == jnp.arange(slots, dtype=jnp.int32)).astype(jnp.bfloat16)
    picked = jnp.einsum("cts,csd->ctd", pick, back, preferred_element_type=jnp.float32)
    combined = (gates_all[:, :, None] * picked).astype(jnp.bfloat16)
    returned = lax.all_to_all(
        combined, "ctx", split_axis=0, concat_axis=0, tiled=True, axis_index_groups=chip_groups
    )
    moe_input_grad = returned.transpose(1, 0, 2).reshape(1, tok_rows, width)
    back_prob = lax.all_to_all(
        slot_prob.reshape(experts, capacity), "exp", split_axis=0, concat_axis=0, tiled=True
    ).reshape(slots)
    prob_grad = back_prob[slot_keys][None, :, None]
    return (moe_input_grad, prob_grad, query_grad[None], kv_grad[None])


def solution(mesh):
    tok = P("exp", "ctx", None)
    placed = (
        tok,
        tok,
        tok,
        P("ctx", "exp", None, None),
        P("exp", None, "ctx"),
        tok,
        tok,
        tok,
        tok,
        tok,
    )
    return jax.shard_map(
        body,
        mesh=mesh,
        in_specs=placed,
        out_specs=(tok, tok, tok, tok),
        check_vma=False,
    )
```

```python
import functools

import jax
import jax.numpy as jnp
from jax import lax
from jax.experimental import pallas as pl
from jax.experimental.pallas import tpu as pltpu
from jax.sharding import PartitionSpec as P

KEY_VALUE_HEADS = 2
HEAD_SIZE = 128
LOG2E = 1.4426950408889634
NT = (((1,), (1,)), ((), ()))


def attention_kernel(
    pairs, pos_ref, q_ref, g_ref, o_ref, kv_ref, dq_ref, out_ref, dkv_ref, kt_ref, bias_ref, st_ref, ds_ref
):
    seq_len = kv_ref.shape[0]
    rows = q_ref.shape[0]
    hd = HEAD_SIZE
    scale = hd**-0.5
    chunk = 256
    chunks = [pl.ds(i * chunk, chunk) for i in range(seq_len // chunk)]

    @pl.when(pl.program_id(1) == 0)
    def _():
        kt_ref[...] = kv_ref[:, :hd].astype(jnp.float32).T.astype(jnp.bfloat16)
        dkv_ref[...] = jnp.zeros_like(dkv_ref)
        key_pos = lax.broadcasted_iota(jnp.int32, bias_ref.shape, 0)
        row_pos = pos_ref[0] + lax.broadcasted_iota(jnp.int32, bias_ref.shape, 1) % rows
        bias_ref[...] = jnp.where(key_pos <= row_pos, 0.0, -1e30).astype(jnp.float32)

    for pair in range(pairs):
        cols = [pl.ds((2 * pair + i) * hd, hd) for i in range(2)]
        q2 = jnp.concatenate([q_ref[:, col] for col in cols], axis=0)
        g2 = jnp.concatenate([g_ref[:, col] for col in cols], axis=0)
        o2 = jnp.concatenate([o_ref[:, col] for col in cols], axis=0)
        prod = g2.astype(jnp.float32) * o2.astype(jnp.float32)
        delta = jnp.sum(prod.T, axis=0, keepdims=True)
        top = jnp.full((1, 2 * rows), -jnp.inf, jnp.float32)
        for part in chunks:
            s = lax.dot_general(kv_ref[part, :hd], q2, NT, preferred_element_type=jnp.float32)
            s = s + bias_ref[part, :]
            st_ref[pair, part, :] = s
            top = jnp.maximum(top, jnp.max(s, axis=0, keepdims=True))
        total = jnp.zeros((1, 2 * rows), jnp.float32)
        for part in chunks:
            e = jnp.exp2((st_ref[pair, part, :] - top) * (scale * LOG2E))
            st_ref[pair, part, :] = e
            total = total + jnp.sum(e, axis=0, keepdims=True)
        inverse = 1.0 / total
        for part in chunks:
            p = st_ref[pair, part, :] * inverse
            dkv_ref[part, hd:] += jnp.dot(
                p.astype(jnp.bfloat16), g2, preferred_element_type=jnp.float32
            )
            dp = lax.dot_general(kv_ref[part, hd:], g2, NT, preferred_element_type=jnp.float32)
            ds = (p * (dp - delta)).astype(jnp.bfloat16)
            ds_ref[pair, part, :] = ds
            dkv_ref[part, :hd] += jnp.dot(ds, q2, preferred_element_type=jnp.float32) * scale
        dqt = jnp.dot(kt_ref[...], ds_ref[pair], preferred_element_type=jnp.float32) * scale
        dq = dqt.T
        for i in range(2):
            dq_ref[:, cols[i]] = dq[i * rows : (i + 1) * rows].astype(dq_ref.dtype)

    @pl.when(pl.program_id(1) == pl.num_programs(1) - 1)
    def _():
        out_ref[...] = dkv_ref[...].astype(out_ref.dtype)


def attention(q, g, o, kv, first):
    rows, width = q.shape
    seq_len = kv.shape[0]
    hd = HEAD_SIZE
    pairs = 2
    step = pairs * 2 * hd
    steps = width // KEY_VALUE_HEADS // step
    tok = pl.BlockSpec((rows, step), lambda h, i: (0, h * steps + i))
    key = pl.BlockSpec((seq_len, 2 * hd), lambda h, i: (0, h))
    return pl.pallas_call(
        functools.partial(attention_kernel, pairs),
        grid=(KEY_VALUE_HEADS, steps),
        in_specs=[pl.BlockSpec(memory_space=pltpu.SMEM), tok, tok, tok, key],
        out_specs=[tok, key],
        out_shape=[
            jax.ShapeDtypeStruct((rows, width), jnp.bfloat16),
            jax.ShapeDtypeStruct((seq_len, kv.shape[1]), jnp.bfloat16),
        ],
        scratch_shapes=[
            pltpu.VMEM((seq_len, 2 * hd), jnp.float32),
            pltpu.VMEM((hd, seq_len), jnp.bfloat16),
            pltpu.VMEM((seq_len, 2 * rows), jnp.float32),
            pltpu.VMEM((pairs, seq_len, 2 * rows), jnp.float32),
            pltpu.VMEM((pairs, seq_len, 2 * rows), jnp.bfloat16),
        ],
        compiler_params=pltpu.CompilerParams(vmem_limit_bytes=40 * 1024 * 1024),
        cost_estimate=pl.CostEstimate(
            flops=10 * rows * seq_len * width,
            bytes_accessed=8 * rows * width + 6 * seq_len * kv.shape[1],
            transcendentals=rows * seq_len * width // hd,
        ),
    )(first, q, g, o, kv)


def body(
    grad_out,
    routes,
    gate_probs,
    saved_pre,
    down_weight,
    gate_up_weight,
    queries,
    keys_values,
    attn_grad,
    attn_out,
):
    experts = lax.axis_size("exp")
    contexts = lax.axis_size("ctx")
    tok_rows = grad_out.shape[1]
    width = grad_out.shape[2]
    capacity = saved_pre.shape[2] // experts
    hidden = down_weight.shape[1]
    chips = contexts // 2
    chip_groups = [[2 * i + core for i in range(chips)] for core in range(2)]

    swap = [(i, i ^ 1) for i in range(contexts)]

    route_rows = routes[0]
    one_hot = (
        route_rows.reshape(-1)[:, None] == jnp.arange(experts, dtype=jnp.int32)[None, :]
    ).astype(jnp.int32)
    earlier = jnp.cumsum(one_hot, axis=0) - one_hot
    positions = jnp.sum(earlier * one_hot, axis=-1)
    slot_keys = route_rows[:, 0] * capacity + positions
    slots = experts * capacity

    kv_local = keys_values[0]
    kv_width = kv_local.shape[1]
    extra = jnp.broadcast_to(
        jnp.pad(slot_keys.astype(jnp.bfloat16), (0, kv_width - tok_rows))[None], (16, kv_width)
    )
    kv_wide = lax.all_gather(jnp.concatenate([kv_local, extra], axis=0), "ctx", axis=0)
    kv_all = kv_wide[:, :tok_rows].reshape(contexts * tok_rows, kv_width)
    block_keys = kv_wide[:, tok_rows, :tok_rows].astype(jnp.int32)
    core = lax.axis_index("ctx") % 2
    block_keys = block_keys.reshape(chips, 2, tok_rows)
    block_keys = jnp.where(core == 0, block_keys[:, 0], block_keys[:, 1])

    down_shard, kv_all = lax.optimization_barrier((down_weight[0], kv_all))
    down_full = lax.all_gather(down_shard, "ctx", axis=1, tiled=True)
    gate_up_own = gate_up_weight[0]
    gate_up_other = lax.ppermute(gate_up_own, "ctx", swap)

    dispatch = (jnp.arange(slots, dtype=jnp.int32)[:, None] == slot_keys[None, :]).astype(
        jnp.bfloat16
    )
    send_rows = jnp.dot(dispatch, grad_out[0], preferred_element_type=jnp.float32).astype(
        jnp.bfloat16
    )
    expert_rows = lax.all_to_all(
        send_rows.reshape(experts, capacity, width), "exp", split_axis=0, concat_axis=0, tiled=True
    ).reshape(slots, width)

    first = (lax.axis_index("ctx") * tok_rows).astype(jnp.int32).reshape(1)
    query_grad, kv_terms = attention(queries[0], attn_grad[0], attn_out[0], kv_all, first)
    kv_back = lax.all_to_all(
        kv_terms.reshape(contexts, tok_rows, kv_width),
        "ctx",
        split_axis=0,
        concat_axis=0,
        tiled=True,
    )

    down_grad = lax.dot_general(expert_rows, down_full, NT, preferred_element_type=jnp.float32)
    pre_acts = saved_pre[0, 0]
    gate_pre = pre_acts[:, :hidden].astype(jnp.float32)
    up_pre = pre_acts[:, hidden:].astype(jnp.float32)
    sigma = jax.nn.sigmoid(gate_pre)
    swish = gate_pre * sigma
    slot_prob = jnp.sum(down_grad * swish * up_pre, axis=-1).astype(jnp.bfloat16)
    gate_part = down_grad * up_pre * sigma * (1.0 + gate_pre * (1.0 - sigma))
    up_part = down_grad * swish
    pre_grad = jnp.concatenate([gate_part, up_part], axis=-1).astype(jnp.bfloat16)

    pre_all = lax.all_gather(pre_grad, "ctx", axis=0, tiled=True, axis_index_groups=chip_groups)
    back_prob = lax.all_to_all(
        slot_prob.reshape(experts, capacity), "exp", split_axis=0, concat_axis=0, tiled=True
    ).reshape(slots)
    pre_all, back_prob, kv_back = lax.optimization_barrier((pre_all, back_prob, kv_back))
    slot_input = jnp.concatenate(
        [
            lax.dot_general(pre_all, part, NT, preferred_element_type=jnp.float32).astype(
                jnp.bfloat16
            )
            for part in (gate_up_own, gate_up_other)
        ],
        axis=1,
    )
    columns = slot_input.shape[1]
    back = lax.all_to_all(
        slot_input.reshape(chips, experts, capacity, columns),
        "exp",
        split_axis=1,
        concat_axis=1,
        tiled=True,
    ).reshape(chips, slots, columns)
    pick = (block_keys[:, :, None] == jnp.arange(slots, dtype=jnp.int32)).astype(jnp.bfloat16)
    picked = jnp.einsum("cts,csd->ctd", pick, back, preferred_element_type=jnp.float32).astype(
        jnp.bfloat16
    )
    returned = lax.all_to_all(
        picked, "ctx", split_axis=0, concat_axis=0, tiled=True, axis_index_groups=chip_groups
    )
    gated = gate_probs[0][None] * returned.astype(jnp.float32)
    gated = gated.astype(jnp.bfloat16).transpose(1, 0, 2).reshape(tok_rows, chips, 2, columns // 2)
    gated = jnp.where(core == 0, gated, gated[:, :, ::-1])
    moe_input_grad = gated.reshape(1, tok_rows, width)
    own_slots = slot_keys[:, None] == jnp.arange(slots, dtype=jnp.int32)
    prob_grad = jnp.sum(
        jnp.where(own_slots, back_prob.astype(jnp.float32), 0.0), axis=1
    ).astype(jnp.bfloat16)[None, :, None]
    kv_grad = jnp.sum(kv_back.astype(jnp.float32), axis=0).astype(jnp.bfloat16)
    return (moe_input_grad, prob_grad, query_grad[None], kv_grad[None])


def solution(mesh):
    tok = P("exp", "ctx", None)
    placed = (
        tok,
        tok,
        tok,
        P("ctx", "exp", None, None),
        P("exp", None, "ctx"),
        tok,
        tok,
        tok,
        tok,
        tok,
    )
    return jax.shard_map(
        body,
        mesh=mesh,
        in_specs=placed,
        out_specs=(tok, tok, tok, tok),
        check_vma=False,
    )
```

```python
import functools

import jax
import jax.numpy as jnp
from jax import lax
from jax.experimental import pallas as pl
from jax.experimental.pallas import tpu as pltpu
from jax.sharding import PartitionSpec as P

KEY_VALUE_HEADS = 2
HEAD_SIZE = 128
LOG2E = 1.4426950408889634
NT = (((1,), (1,)), ((), ()))


def attention_kernel(
    pairs, pos_ref, q_ref, g_ref, o_ref, kv_ref, dq_ref, out_ref, dkv_ref, kt_ref, bias_ref, st_ref, ds_ref
):
    seq_len = kv_ref.shape[0]
    rows = q_ref.shape[0]
    hd = HEAD_SIZE
    scale = hd**-0.5
    chunk = 256
    chunks = [pl.ds(i * chunk, chunk) for i in range(seq_len // chunk)]

    @pl.when(pl.program_id(1) == 0)
    def _():
        kt_ref[...] = kv_ref[:, :hd].astype(jnp.float32).T.astype(jnp.bfloat16)
        dkv_ref[...] = jnp.zeros_like(dkv_ref)
        key_pos = lax.broadcasted_iota(jnp.int32, bias_ref.shape, 0)
        row_pos = pos_ref[0] + lax.broadcasted_iota(jnp.int32, bias_ref.shape, 1) % rows
        bias_ref[...] = jnp.where(key_pos <= row_pos, 0.0, -1e30).astype(jnp.float32)

    for pair in range(pairs):
        cols = [pl.ds((2 * pair + i) * hd, hd) for i in range(2)]
        q2 = jnp.concatenate([q_ref[:, col] for col in cols], axis=0)
        g2 = jnp.concatenate([g_ref[:, col] for col in cols], axis=0)
        o2 = jnp.concatenate([o_ref[:, col] for col in cols], axis=0)
        prod = g2.astype(jnp.float32) * o2.astype(jnp.float32)
        delta = jnp.sum(prod.T, axis=0, keepdims=True)
        top = jnp.full((1, 2 * rows), -jnp.inf, jnp.float32)
        for part in chunks:
            s = lax.dot_general(kv_ref[part, :hd], q2, NT, preferred_element_type=jnp.float32)
            s = s + bias_ref[part, :]
            st_ref[pair, part, :] = s
            top = jnp.maximum(top, jnp.max(s, axis=0, keepdims=True))
        total = jnp.zeros((1, 2 * rows), jnp.float32)
        for part in chunks:
            e = jnp.exp2((st_ref[pair, part, :] - top) * (scale * LOG2E))
            st_ref[pair, part, :] = e
            total = total + jnp.sum(e, axis=0, keepdims=True)
        inverse = 1.0 / total
        for part in chunks:
            p = st_ref[pair, part, :] * inverse
            dkv_ref[part, hd:] += jnp.dot(
                p.astype(jnp.bfloat16), g2, preferred_element_type=jnp.float32
            )
            dp = lax.dot_general(kv_ref[part, hd:], g2, NT, preferred_element_type=jnp.float32)
            ds = (p * (dp - delta)).astype(jnp.bfloat16)
            ds_ref[pair, part, :] = ds
            dkv_ref[part, :hd] += jnp.dot(ds, q2, preferred_element_type=jnp.float32) * scale
        dqt = jnp.dot(kt_ref[...], ds_ref[pair], preferred_element_type=jnp.float32) * scale
        dq = dqt.T
        for i in range(2):
            dq_ref[:, cols[i]] = dq[i * rows : (i + 1) * rows].astype(dq_ref.dtype)

    @pl.when(pl.program_id(1) == pl.num_programs(1) - 1)
    def _():
        out_ref[...] = dkv_ref[...].astype(out_ref.dtype)


def attention(q, g, o, kv, first):
    rows, width = q.shape
    seq_len = kv.shape[0]
    hd = HEAD_SIZE
    pairs = 2
    step = pairs * 2 * hd
    steps = width // KEY_VALUE_HEADS // step
    tok = pl.BlockSpec((rows, step), lambda h, i: (0, h * steps + i))
    key = pl.BlockSpec((seq_len, 2 * hd), lambda h, i: (0, h))
    return pl.pallas_call(
        functools.partial(attention_kernel, pairs),
        grid=(KEY_VALUE_HEADS, steps),
        in_specs=[pl.BlockSpec(memory_space=pltpu.SMEM), tok, tok, tok, key],
        out_specs=[tok, key],
        out_shape=[
            jax.ShapeDtypeStruct((rows, width), jnp.bfloat16),
            jax.ShapeDtypeStruct((seq_len, kv.shape[1]), jnp.bfloat16),
        ],
        scratch_shapes=[
            pltpu.VMEM((seq_len, 2 * hd), jnp.float32),
            pltpu.VMEM((hd, seq_len), jnp.bfloat16),
            pltpu.VMEM((seq_len, 2 * rows), jnp.float32),
            pltpu.VMEM((pairs, seq_len, 2 * rows), jnp.float32),
            pltpu.VMEM((pairs, seq_len, 2 * rows), jnp.bfloat16),
        ],
        compiler_params=pltpu.CompilerParams(vmem_limit_bytes=40 * 1024 * 1024),
        cost_estimate=pl.CostEstimate(
            flops=10 * rows * seq_len * width,
            bytes_accessed=8 * rows * width + 6 * seq_len * kv.shape[1],
            transcendentals=rows * seq_len * width // hd,
        ),
    )(first, q, g, o, kv)


MESH = pl.DeviceIdType.MESH


def return_kernel(
    chips,
    experts,
    pre_ref,
    gu_ref,
    pick_ref,
    gate_ref,
    out_ref,
    pre_buf,
    gu_buf,
    sent,
    came,
    leaving,
    landed,
    pair_sems,
    up_sems,
    down_sems,
    pre_sems,
    cross_out,
    cross_in,
    back_out,
    back_in,
):
    me = lax.axis_index("ctx")
    mine = lax.axis_index("exp")
    z = lax.div(me, 2)
    core = lax.rem(me, 2)
    shard = gu_ref.shape[0]
    columns = 2 * shard
    tile = min(shard, 256)

    barrier = pltpu.get_barrier_semaphore()
    for d in range(1, chips):
        chip = lax.rem(z + d, chips)
        pl.semaphore_signal(
            barrier, inc=1, device_id={"ctx": 2 * chip + core}, device_id_type=MESH
        )
    for d in range(1, experts):
        pl.semaphore_signal(
            barrier, inc=1, device_id={"exp": lax.rem(mine + d, experts)}, device_id_type=MESH
        )
    other = 2 * z + 1 - core
    pl.semaphore_signal(barrier, inc=1, device_id={"ctx": other}, device_id_type=MESH)
    pre_buf[z] = pre_ref[...]
    pl.semaphore_wait(barrier, chips + experts - 1)

    def remote(src, dst, send, recv, device):
        return pltpu.make_async_remote_copy(
            src_ref=src,
            dst_ref=dst,
            send_sem=send,
            recv_sem=recv,
            device_id=device,
            device_id_type=MESH,
        )

    def up(b):
        return remote(
            pre_buf.at[b], pre_buf.at[b], up_sems.at[b], pre_sems.at[b], {"ctx": me + 2}
        )

    def down(b):
        return remote(
            pre_buf.at[b], pre_buf.at[b], down_sems.at[b], pre_sems.at[b], {"ctx": me - 2}
        )

    def cross(b, to, slot):
        return remote(
            sent.at[b, to], came.at[b, slot], cross_out.at[b, to], cross_in.at[b, slot], {"exp": to}
        )

    def back(b, slot):
        return remote(
            leaving.at[b],
            landed.at[slot],
            back_out.at[b],
            back_in.at[slot],
            {"ctx": 2 * b + core},
        )

    swap = remote(
        gu_ref, gu_buf.at[core], pair_sems.at[0], pair_sems.at[1], {"ctx": other}
    )
    has_up = z + 1 < chips
    has_down = z > 0

    @pl.when(has_up)
    def _():
        up(z).start()

    @pl.when(has_down)
    def _():
        down(z).start()

    swap.start()
    gu_buf[core] = gu_ref[...]
    swap.wait_recv()

    def block_of(i):
        ahead = lax.rem(z + i, chips)
        behind = lax.rem(z - i + chips, chips)
        return jnp.where(z < chips // 2, ahead, behind)

    def combine(b):
        for d in range(1, experts):
            j = lax.rem(mine + d, experts)
            cross(b, j, j).wait_recv()
        slots = pick_ref.shape[2]
        for t in range(columns // tile):
            cols = pl.ds(t * tile, tile)
            rows = came[b, :, :, cols].reshape(slots, tile)
            leaving[b, :, cols] = jnp.dot(
                pick_ref[b], rows, preferred_element_type=jnp.float32
            ).astype(leaving.dtype)

        @pl.when(b != z)
        def _():
            back(b, z).start()

        @pl.when(b == z)
        def _():
            landed[z] = leaving[b]

    def turn(i, carry):
        lo = z - i
        hi = z + i

        @pl.when((i > 0) & (lo >= 0))
        def _():
            up(lo).wait_recv()

            @pl.when(has_up)
            def _():
                up(lo).start()

        @pl.when((i > 0) & (hi < chips))
        def _():
            down(hi).wait_recv()

            @pl.when(has_down)
            def _():
                down(hi).start()

        b = block_of(i)
        for half in range(2):
            for t in range(shard // tile):
                weights = gu_buf[half, pl.ds(t * tile, tile), :]
                grads = lax.dot_general(
                    pre_buf[b], weights, NT, preferred_element_type=jnp.float32
                )
                cols = pl.ds(half * shard + t * tile, tile)
                sent[b, :, :, cols] = grads.astype(sent.dtype).reshape(experts, -1, tile)
        for d in range(1, experts):
            cross(b, lax.rem(mine + d, experts), mine).start()
        came[b, mine] = sent[b, mine]

        @pl.when(i > 0)
        def _():
            combine(block_of(i - 1))

        return carry

    lax.fori_loop(0, chips, turn, 0)
    combine(block_of(chips - 1))
    for b in range(chips):

        @pl.when(z != b)
        def _():
            back(b, b).wait_recv()

        out_ref[:, pl.ds(b * columns, columns)] = (
            gate_ref[...] * landed[b].astype(jnp.float32)
        ).astype(out_ref.dtype)

    swap.wait_send()
    for b in range(chips):

        @pl.when(has_up & (z >= b))
        def _():
            up(b).wait_send()

        @pl.when(has_down & (z <= b))
        def _():
            down(b).wait_send()

        @pl.when(z != b)
        def _():
            back(b, z).wait_send()

        for d in range(1, experts):
            cross(b, lax.rem(mine + d, experts), mine).wait_send()


def expert_return(pre_grad, gate_up, pick, gates, chips, experts):
    slots, pre_width = pre_grad.shape
    capacity = slots // experts
    shard = gate_up.shape[0]
    tok_rows = gates.shape[0]
    columns = 2 * shard
    vmem = pl.BlockSpec(memory_space=pltpu.VMEM)
    low = jnp.bfloat16
    dma = pltpu.SemaphoreType.DMA
    return pl.pallas_call(
        functools.partial(return_kernel, chips, experts),
        in_specs=[vmem] * 4,
        out_specs=vmem,
        out_shape=jax.ShapeDtypeStruct((tok_rows, chips * columns), low),
        scratch_shapes=[
            pltpu.VMEM((chips, slots, pre_width), low),
            pltpu.VMEM((2, shard, pre_width), low),
            pltpu.VMEM((chips, experts, capacity, columns), low),
            pltpu.VMEM((chips, experts, capacity, columns), low),
            pltpu.VMEM((chips, tok_rows, columns), low),
            pltpu.VMEM((chips, tok_rows, columns), low),
            dma((2,)),
            dma((chips,)),
            dma((chips,)),
            dma((chips,)),
            dma((chips, experts)),
            dma((chips, experts)),
            dma((chips,)),
            dma((chips,)),
        ],
        compiler_params=pltpu.CompilerParams(
            collective_id=0, has_side_effects=True, vmem_limit_bytes=40 * 1024 * 1024
        ),
        cost_estimate=pl.CostEstimate(
            flops=2 * chips * slots * pre_width * columns,
            bytes_accessed=4 * (slots * pre_width + shard * pre_width),
            transcendentals=0,
        ),
    )(pre_grad, gate_up, pick, gates)


def body(
    grad_out,
    routes,
    gate_probs,
    saved_pre,
    down_weight,
    gate_up_weight,
    queries,
    keys_values,
    attn_grad,
    attn_out,
):
    experts = lax.axis_size("exp")
    contexts = lax.axis_size("ctx")
    tok_rows = grad_out.shape[1]
    width = grad_out.shape[2]
    filled = saved_pre.shape[2] // experts
    capacity = -(-filled // 16) * 16
    hidden = down_weight.shape[1]
    chips = contexts // 2

    route_rows = routes[0]
    one_hot = (
        route_rows.reshape(-1)[:, None] == jnp.arange(experts, dtype=jnp.int32)[None, :]
    ).astype(jnp.int32)
    earlier = jnp.cumsum(one_hot, axis=0) - one_hot
    positions = jnp.sum(earlier * one_hot, axis=-1)
    slot_keys = route_rows[:, 0] * capacity + positions
    slots = experts * capacity

    kv_local = keys_values[0]
    kv_width = kv_local.shape[1]
    extra = jnp.broadcast_to(
        jnp.pad(slot_keys.astype(jnp.bfloat16), (0, kv_width - tok_rows))[None], (16, kv_width)
    )
    kv_wide = lax.all_gather(jnp.concatenate([kv_local, extra], axis=0), "ctx", axis=0)
    kv_all = kv_wide[:, :tok_rows].reshape(contexts * tok_rows, kv_width)
    block_keys = kv_wide[:, tok_rows, :tok_rows].astype(jnp.int32)
    core = lax.axis_index("ctx") % 2
    block_keys = block_keys.reshape(chips, 2, tok_rows)
    block_keys = jnp.where(core == 0, block_keys[:, 0], block_keys[:, 1])

    down_shard, kv_all = lax.optimization_barrier((down_weight[0], kv_all))
    down_full = lax.all_gather(down_shard, "ctx", axis=1, tiled=True)

    dispatch = (jnp.arange(slots, dtype=jnp.int32)[:, None] == slot_keys[None, :]).astype(
        jnp.bfloat16
    )
    send_rows = jnp.dot(dispatch, grad_out[0], preferred_element_type=jnp.float32).astype(
        jnp.bfloat16
    )
    expert_rows = lax.all_to_all(
        send_rows.reshape(experts, capacity, width), "exp", split_axis=0, concat_axis=0, tiled=True
    ).reshape(slots, width)

    first = (lax.axis_index("ctx") * tok_rows).astype(jnp.int32).reshape(1)
    query_grad, kv_terms = attention(queries[0], attn_grad[0], attn_out[0], kv_all, first)
    kv_back = lax.all_to_all(
        kv_terms.reshape(contexts, tok_rows, kv_width),
        "ctx",
        split_axis=0,
        concat_axis=0,
        tiled=True,
    )

    down_grad = lax.dot_general(expert_rows, down_full, NT, preferred_element_type=jnp.float32)
    pre_acts = saved_pre[0, 0]
    if capacity != filled:
        pre_acts = pre_acts.reshape(experts, filled, 2 * hidden)
        pre_acts = jnp.pad(pre_acts, ((0, 0), (0, capacity - filled), (0, 0)))
        pre_acts = pre_acts.reshape(slots, 2 * hidden)
    gate_pre = pre_acts[:, :hidden].astype(jnp.float32)
    up_pre = pre_acts[:, hidden:].astype(jnp.float32)
    sigma = jax.nn.sigmoid(gate_pre)
    swish = gate_pre * sigma
    slot_prob = jnp.sum(down_grad * swish * up_pre, axis=-1).astype(jnp.bfloat16)
    gate_part = down_grad * up_pre * sigma * (1.0 + gate_pre * (1.0 - sigma))
    up_part = down_grad * swish
    pre_grad = jnp.concatenate([gate_part, up_part], axis=-1).astype(jnp.bfloat16)

    back_prob = lax.all_to_all(
        slot_prob.reshape(experts, capacity), "exp", split_axis=0, concat_axis=0, tiled=True
    ).reshape(slots)
    pre_grad, back_prob, kv_back = lax.optimization_barrier((pre_grad, back_prob, kv_back))
    pick = (block_keys[:, :, None] == jnp.arange(slots, dtype=jnp.int32)).astype(jnp.bfloat16)
    moe_input_grad = expert_return(
        pre_grad, gate_up_weight[0], pick, gate_probs[0], chips, experts
    )[None]
    own_slots = slot_keys[:, None] == jnp.arange(slots, dtype=jnp.int32)
    prob_grad = jnp.sum(
        jnp.where(own_slots, back_prob.astype(jnp.float32), 0.0), axis=1
    ).astype(jnp.bfloat16)[None, :, None]
    kv_grad = jnp.sum(kv_back.astype(jnp.float32), axis=0).astype(jnp.bfloat16)
    return (moe_input_grad, prob_grad, query_grad[None], kv_grad[None])


def solution(mesh):
    tok = P("exp", "ctx", None)
    placed = (
        tok,
        tok,
        tok,
        P("ctx", "exp", None, None),
        P("exp", None, "ctx"),
        tok,
        tok,
        tok,
        tok,
        tok,
    )
    return jax.shard_map(
        body,
        mesh=mesh,
        in_specs=placed,
        out_specs=(tok, tok, tok, tok),
        check_vma=False,
    )
```

```python
import functools

import jax
import jax.numpy as jnp
from jax import lax
from jax.experimental import pallas as pl
from jax.experimental.pallas import tpu as pltpu
from jax.sharding import PartitionSpec as P

KEY_VALUE_HEADS = 2
HEAD_SIZE = 128
LOG2E = 1.4426950408889634
NT = (((1,), (1,)), ((), ()))


MESH = pl.DeviceIdType.MESH


def gather_kernel(
    chips,
    experts,
    kv_ref,
    down_ref,
    rows_ref,
    q_ref,
    g_ref,
    o_ref,
    dq_ref,
    kv_grad_ref,
    hidden_ref,
    extra_ref,
    kv_buf,
    down_buf,
    row_buf,
    kv_all,
    terms,
    keys_t,
    bias,
    scores,
    low_grads,
    pair_terms,
    leaving,
    landed,
    kv_up,
    kv_down,
    kv_in,
    kv_swap_out,
    kv_swap_in,
    w_up,
    w_down,
    w_in,
    w_swap_out,
    w_swap_in,
    row_out,
    row_in,
    pair_out,
    pair_in,
    term_out,
    term_in,
):
    me = lax.axis_index("ctx")
    mine = lax.axis_index("exp")
    z = lax.div(me, 2)
    core = lax.rem(me, 2)
    partner = 2 * z + 1 - core
    tok_rows, width = q_ref.shape
    seq_len = kv_all.shape[0]
    hd = HEAD_SIZE
    has_up = z + 1 < chips
    has_down = z > 0

    barrier = pltpu.get_barrier_semaphore()
    for d in range(1, chips):
        chip = lax.rem(z + d, chips)
        pl.semaphore_signal(
            barrier, inc=1, device_id={"ctx": 2 * chip + core}, device_id_type=MESH
        )
    for d in range(1, experts):
        pl.semaphore_signal(
            barrier, inc=1, device_id={"exp": lax.rem(mine + d, experts)}, device_id_type=MESH
        )
    pl.semaphore_signal(barrier, inc=1, device_id={"ctx": partner}, device_id_type=MESH)
    kv_buf[z, core] = kv_ref[...]
    down_buf[z, core] = down_ref[...]
    pl.semaphore_wait(barrier, chips + experts - 1)

    def remote(src, dst, send, recv, device):
        return pltpu.make_async_remote_copy(
            src_ref=src,
            dst_ref=dst,
            send_sem=send,
            recv_sem=recv,
            device_id=device,
            device_id_type=MESH,
        )

    class Line:
        def __init__(self, buf, up, down, arrived, swap_out, swap_in):
            self.buf, self.sems = buf, (up, down, arrived, swap_out, swap_in)

        def up(self, b):
            ref = self.buf.at[b, core]
            return remote(ref, ref, self.sems[0].at[b], self.sems[2].at[b], {"ctx": me + 2})

        def down(self, b):
            ref = self.buf.at[b, core]
            return remote(ref, ref, self.sems[1].at[b], self.sems[2].at[b], {"ctx": me - 2})

        def swap(self, b, side):
            ref = self.buf.at[b, side]
            return remote(ref, ref, self.sems[3].at[b], self.sems[4].at[b], {"ctx": partner})

        def begin(self):
            @pl.when(has_up)
            def _():
                self.up(z).start()

            @pl.when(has_down)
            def _():
                self.down(z).start()

            self.swap(z, core).start()

        def relay(self, i, on=True):
            lo = z - i
            hi = z + i

            @pl.when((lo >= 0) & on)
            def _():
                self.up(lo).wait_recv()

                @pl.when(has_up)
                def _():
                    self.up(lo).start()

                self.swap(lo, core).start()

            @pl.when((hi < chips) & on)
            def _():
                self.down(hi).wait_recv()

                @pl.when(has_down)
                def _():
                    self.down(hi).start()

                self.swap(hi, core).start()

        def finish(self):
            for b in range(chips):

                @pl.when(has_up & (z >= b))
                def _():
                    self.up(b).wait_send()

                @pl.when(has_down & (z <= b))
                def _():
                    self.down(b).wait_send()

                self.swap(b, core).wait_send()

    kv_line = Line(kv_buf, kv_up, kv_down, kv_in, kv_swap_out, kv_swap_in)
    w_line = Line(down_buf, w_up, w_down, w_in, w_swap_out, w_swap_in)

    def cross(to, slot):
        return remote(
            rows_ref.at[to], row_buf.at[slot], row_out.at[to], row_in.at[slot], {"exp": to}
        )

    kv_line.begin()
    w_line.begin()
    for d in range(1, experts):
        cross(lax.rem(mine + d, experts), mine).start()
    row_buf[mine] = rows_ref[mine]

    terms[...] = jnp.zeros_like(terms)
    key_pos = lax.broadcasted_iota(jnp.int32, bias.shape, 0)
    row_pos = me * tok_rows + lax.rem(lax.broadcasted_iota(jnp.int32, bias.shape, 1), tok_rows)
    bias[...] = jnp.where(key_pos <= row_pos, 0.0, -1e30).astype(jnp.float32)
    for i in range(1, chips):
        kv_line.relay(i)
    for b in range(chips):
        kv_line.swap(b, 1 - core).wait_recv()
        for side in range(2):
            kv_all[pl.ds((2 * b + side) * tok_rows, tok_rows), :] = kv_buf[b, side, :tok_rows, :]
        extra_ref[b] = kv_buf[b, core, tok_rows:, :]
    for head in range(KEY_VALUE_HEADS):
        keys = kv_all[:, 2 * hd * head : 2 * hd * head + hd]
        keys_t[head] = keys.astype(jnp.float32).T.astype(jnp.bfloat16)

    scale = hd**-0.5
    chunk = 256
    chunks = [pl.ds(i * chunk, chunk) for i in range(seq_len // chunk)]
    pairs = scores.shape[0]
    step = 2 * pairs * hd
    units = width // step

    def unit(u, carry):
        for i in range(1, min(chips, 3)):

            @pl.when(u == (units - 2) * (i - 1) + 1)
            def _():
                w_line.relay(i)

        head = lax.div(u, units // KEY_VALUE_HEADS)
        key_cols = pl.ds(pl.multiple_of(head * 2 * hd, hd), hd)
        val_cols = pl.ds(pl.multiple_of(head * 2 * hd + hd, hd), hd)
        for pair in range(pairs):
            cols = [
                pl.ds(pl.multiple_of(u * step + (2 * pair + i) * hd, hd), hd) for i in range(2)
            ]
            q2 = jnp.concatenate([q_ref[:, col] for col in cols], axis=0)
            g2 = jnp.concatenate([g_ref[:, col] for col in cols], axis=0)
            o2 = jnp.concatenate([o_ref[:, col] for col in cols], axis=0)
            prod = g2.astype(jnp.float32) * o2.astype(jnp.float32)
            delta = jnp.sum(prod.T, axis=0, keepdims=True)
            top = jnp.full((1, 2 * tok_rows), -jnp.inf, jnp.float32)
            for part in chunks:
                s = lax.dot_general(
                    kv_all[part, key_cols], q2, NT, preferred_element_type=jnp.float32
                )
                s = s + bias[part, :]
                scores[pair, part, :] = s
                top = jnp.maximum(top, jnp.max(s, axis=0, keepdims=True))
            total = jnp.zeros((1, 2 * tok_rows), jnp.float32)
            for part in chunks:
                e = jnp.exp2((scores[pair, part, :] - top) * (scale * LOG2E))
                scores[pair, part, :] = e
                total = total + jnp.sum(e, axis=0, keepdims=True)
            inverse = 1.0 / total
            for part in chunks:
                p = scores[pair, part, :] * inverse
                terms[part, val_cols] += jnp.dot(
                    p.astype(jnp.bfloat16), g2, preferred_element_type=jnp.float32
                )
                dp = lax.dot_general(
                    kv_all[part, val_cols], g2, NT, preferred_element_type=jnp.float32
                )
                ds = (p * (dp - delta)).astype(jnp.bfloat16)
                low_grads[pair, part, :] = ds
                terms[part, key_cols] += (
                    jnp.dot(ds, q2, preferred_element_type=jnp.float32) * scale
                )
            dq = (
                jnp.dot(keys_t[head], low_grads[pair], preferred_element_type=jnp.float32) * scale
            ).T
            for i in range(2):
                dq_ref[:, cols[i]] = dq[i * tok_rows : (i + 1) * tok_rows].astype(dq_ref.dtype)
        return carry

    lax.fori_loop(0, units, unit, 0)

    def rows_of(b, side):
        return pl.ds(pl.multiple_of((2 * b + side) * tok_rows, tok_rows), tok_rows)

    def pair_copy(b, side):
        return remote(
            terms.at[rows_of(b, side), :],
            pair_terms.at[b],
            pair_out.at[b],
            pair_in.at[b],
            {"ctx": partner},
        )

    def term_copy(b, slot):
        return remote(
            leaving.at[b],
            landed.at[slot],
            term_out.at[b],
            term_in.at[slot],
            {"ctx": 2 * b + core},
        )

    for b in range(chips):

        @pl.when(b <= z)
        def _():
            pair_copy(b, 1 - core).start()

    for d in range(1, experts):
        j = lax.rem(mine + d, experts)
        cross(j, j).wait_recv()
    hidden_ref[...] = jnp.zeros_like(hidden_ref)
    shard = down_ref.shape[1]
    tile = 256
    slots = hidden_ref.shape[0]

    def hidden_part(i):
        w_line.relay(i, i >= 3)
        ahead = lax.rem(z + i, chips)
        behind = lax.rem(z - i + chips, chips)
        b = jnp.where(z < chips // 2, ahead, behind)
        w_line.swap(b, 1 - core).wait_recv()
        for side in range(2):
            cols = pl.ds(pl.multiple_of((2 * b + side) * shard, shard), shard)
            rows = row_buf[:, :, cols].reshape(slots, shard)
            for t in range(hidden_ref.shape[1] // tile):
                part = pl.ds(t * tile, tile)
                hidden_ref[:, part] += lax.dot_general(
                    rows, down_buf[b, side, part, :], NT, preferred_element_type=jnp.float32
                )

    def hidden_turn(i, carry):
        hidden_part(i)
        return carry

    lax.fori_loop(0, chips - 1, hidden_turn, 0)

    for b in range(chips):

        @pl.when(b <= z)
        def _():
            pair_copy(b, core).wait_recv()

        @pl.when(b < z)
        def _():
            leaving[b] = (terms[rows_of(b, core), :] + pair_terms[b]).astype(leaving.dtype)
            term_copy(b, z).start()

    hidden_part(chips - 1)

    landed_sum = terms[rows_of(z, core), :] + pair_terms[z]
    kv_sum = pair_terms.at[z]
    kv_sum[...] = landed_sum
    for b in range(chips):

        @pl.when(b > z)
        def _():
            term_copy(b, b).wait_recv()
            kv_sum[...] += landed[b].astype(jnp.float32)

    kv_grad_ref[...] = kv_sum[...].astype(kv_grad_ref.dtype)

    kv_line.finish()
    w_line.finish()
    for d in range(1, experts):
        cross(lax.rem(mine + d, experts), mine).wait_send()
    for b in range(chips):

        @pl.when(b <= z)
        def _():
            pair_copy(b, 1 - core).wait_send()

        @pl.when(b < z)
        def _():
            term_copy(b, z).wait_send()


def gather_and_attend(kv_local, down, rows, q, g, o, chips):
    experts, capacity, width = rows.shape
    tok_rows = q.shape[0]
    kv_width = kv_local.shape[1]
    contexts = 2 * chips
    seq_len = contexts * tok_rows
    hidden = down.shape[0]
    hd = HEAD_SIZE
    pairs = 2
    vmem = pl.BlockSpec(memory_space=pltpu.VMEM)
    low, full = jnp.bfloat16, jnp.float32
    dma = pltpu.SemaphoreType.DMA
    per_chip = dma((chips,))
    extra = kv_local.shape[0] - tok_rows
    return pl.pallas_call(
        functools.partial(gather_kernel, chips, experts),
        in_specs=[vmem] * 6,
        out_specs=[vmem] * 4,
        out_shape=[
            jax.ShapeDtypeStruct((tok_rows, width), low),
            jax.ShapeDtypeStruct((tok_rows, kv_width), low),
            jax.ShapeDtypeStruct((experts * capacity, hidden), full),
            jax.ShapeDtypeStruct((chips, extra, kv_width), low),
        ],
        scratch_shapes=[
            pltpu.VMEM((chips, 2) + kv_local.shape, low),
            pltpu.VMEM((chips, 2) + down.shape, low),
            pltpu.VMEM((experts, capacity, width), low),
            pltpu.VMEM((seq_len, kv_width), low),
            pltpu.VMEM((seq_len, kv_width), full),
            pltpu.VMEM((KEY_VALUE_HEADS, hd, seq_len), low),
            pltpu.VMEM((seq_len, 2 * tok_rows), full),
            pltpu.VMEM((pairs, seq_len, 2 * tok_rows), full),
            pltpu.VMEM((pairs, seq_len, 2 * tok_rows), low),
            pltpu.VMEM((chips, tok_rows, kv_width), full),
            pltpu.VMEM((chips, tok_rows, kv_width), low),
            pltpu.VMEM((chips, tok_rows, kv_width), low),
        ]
        + [per_chip] * 10
        + [dma((experts,))] * 2
        + [per_chip] * 4,
        compiler_params=pltpu.CompilerParams(
            collective_id=1, has_side_effects=True, vmem_limit_bytes=52 * 1024 * 1024
        ),
        cost_estimate=pl.CostEstimate(
            flops=10 * tok_rows * seq_len * width,
            bytes_accessed=8 * tok_rows * width,
            transcendentals=tok_rows * seq_len * width // hd,
        ),
    )(kv_local, down, rows, q, g, o)


def return_kernel(
    chips,
    experts,
    pre_ref,
    gu_ref,
    pick_ref,
    gate_ref,
    out_ref,
    pre_buf,
    gu_buf,
    sent,
    came,
    leaving,
    landed,
    pair_sems,
    up_sems,
    down_sems,
    pre_sems,
    cross_out,
    cross_in,
    back_out,
    back_in,
):
    me = lax.axis_index("ctx")
    mine = lax.axis_index("exp")
    z = lax.div(me, 2)
    core = lax.rem(me, 2)
    shard = gu_ref.shape[0]
    columns = 2 * shard
    tile = min(shard, 256)

    barrier = pltpu.get_barrier_semaphore()
    for d in range(1, chips):
        chip = lax.rem(z + d, chips)
        pl.semaphore_signal(
            barrier, inc=1, device_id={"ctx": 2 * chip + core}, device_id_type=MESH
        )
    for d in range(1, experts):
        pl.semaphore_signal(
            barrier, inc=1, device_id={"exp": lax.rem(mine + d, experts)}, device_id_type=MESH
        )
    other = 2 * z + 1 - core
    pl.semaphore_signal(barrier, inc=1, device_id={"ctx": other}, device_id_type=MESH)
    pre_buf[z] = pre_ref[...]
    pl.semaphore_wait(barrier, chips + experts - 1)

    def remote(src, dst, send, recv, device):
        return pltpu.make_async_remote_copy(
            src_ref=src,
            dst_ref=dst,
            send_sem=send,
            recv_sem=recv,
            device_id=device,
            device_id_type=MESH,
        )

    def up(b):
        return remote(
            pre_buf.at[b], pre_buf.at[b], up_sems.at[b], pre_sems.at[b], {"ctx": me + 2}
        )

    def down(b):
        return remote(
            pre_buf.at[b], pre_buf.at[b], down_sems.at[b], pre_sems.at[b], {"ctx": me - 2}
        )

    def cross(b, to, slot):
        return remote(
            sent.at[b, to], came.at[b, slot], cross_out.at[b, to], cross_in.at[b, slot], {"exp": to}
        )

    def back(b, slot):
        return remote(
            leaving.at[b],
            landed.at[slot],
            back_out.at[b],
            back_in.at[slot],
            {"ctx": 2 * b + core},
        )

    swap = remote(
        gu_ref, gu_buf.at[core], pair_sems.at[0], pair_sems.at[1], {"ctx": other}
    )
    has_up = z + 1 < chips
    has_down = z > 0

    @pl.when(has_up)
    def _():
        up(z).start()

    @pl.when(has_down)
    def _():
        down(z).start()

    swap.start()
    gu_buf[core] = gu_ref[...]
    swap.wait_recv()

    def block_of(i):
        ahead = lax.rem(z + i, chips)
        behind = lax.rem(z - i + chips, chips)
        return jnp.where(z < chips // 2, ahead, behind)

    def combine(b):
        for d in range(1, experts):
            j = lax.rem(mine + d, experts)
            cross(b, j, j).wait_recv()
        slots = pick_ref.shape[2]
        for t in range(columns // tile):
            cols = pl.ds(t * tile, tile)
            rows = came[b, :, :, cols].reshape(slots, tile)
            leaving[b, :, cols] = jnp.dot(
                pick_ref[b], rows, preferred_element_type=jnp.float32
            ).astype(leaving.dtype)

        @pl.when(b != z)
        def _():
            back(b, z).start()

        @pl.when(b == z)
        def _():
            landed[z] = leaving[b]

    def turn(i, carry):
        lo = z - i
        hi = z + i

        @pl.when((i > 0) & (lo >= 0))
        def _():
            up(lo).wait_recv()

            @pl.when(has_up)
            def _():
                up(lo).start()

        @pl.when((i > 0) & (hi < chips))
        def _():
            down(hi).wait_recv()

            @pl.when(has_down)
            def _():
                down(hi).start()

        b = block_of(i)
        for half in range(2):
            for t in range(shard // tile):
                weights = gu_buf[half, pl.ds(t * tile, tile), :]
                grads = lax.dot_general(
                    pre_buf[b], weights, NT, preferred_element_type=jnp.float32
                )
                cols = pl.ds(half * shard + t * tile, tile)
                sent[b, :, :, cols] = grads.astype(sent.dtype).reshape(experts, -1, tile)
        for d in range(1, experts):
            cross(b, lax.rem(mine + d, experts), mine).start()
        came[b, mine] = sent[b, mine]

        @pl.when(i > 0)
        def _():
            combine(block_of(i - 1))

        return carry

    lax.fori_loop(0, chips, turn, 0)
    combine(block_of(chips - 1))
    for b in range(chips):

        @pl.when(z != b)
        def _():
            back(b, b).wait_recv()

        out_ref[:, pl.ds(b * columns, columns)] = (
            gate_ref[...] * landed[b].astype(jnp.float32)
        ).astype(out_ref.dtype)

    swap.wait_send()
    for b in range(chips):

        @pl.when(has_up & (z >= b))
        def _():
            up(b).wait_send()

        @pl.when(has_down & (z <= b))
        def _():
            down(b).wait_send()

        @pl.when(z != b)
        def _():
            back(b, z).wait_send()

        for d in range(1, experts):
            cross(b, lax.rem(mine + d, experts), mine).wait_send()


def expert_return(pre_grad, gate_up, pick, gates, chips, experts):
    slots, pre_width = pre_grad.shape
    capacity = slots // experts
    shard = gate_up.shape[0]
    tok_rows = gates.shape[0]
    columns = 2 * shard
    vmem = pl.BlockSpec(memory_space=pltpu.VMEM)
    low = jnp.bfloat16
    dma = pltpu.SemaphoreType.DMA
    return pl.pallas_call(
        functools.partial(return_kernel, chips, experts),
        in_specs=[vmem] * 4,
        out_specs=vmem,
        out_shape=jax.ShapeDtypeStruct((tok_rows, chips * columns), low),
        scratch_shapes=[
            pltpu.VMEM((chips, slots, pre_width), low),
            pltpu.VMEM((2, shard, pre_width), low),
            pltpu.VMEM((chips, experts, capacity, columns), low),
            pltpu.VMEM((chips, experts, capacity, columns), low),
            pltpu.VMEM((chips, tok_rows, columns), low),
            pltpu.VMEM((chips, tok_rows, columns), low),
            dma((2,)),
            dma((chips,)),
            dma((chips,)),
            dma((chips,)),
            dma((chips, experts)),
            dma((chips, experts)),
            dma((chips,)),
            dma((chips,)),
        ],
        compiler_params=pltpu.CompilerParams(
            collective_id=0, has_side_effects=True, vmem_limit_bytes=40 * 1024 * 1024
        ),
        cost_estimate=pl.CostEstimate(
            flops=2 * chips * slots * pre_width * columns,
            bytes_accessed=4 * (slots * pre_width + shard * pre_width),
            transcendentals=0,
        ),
    )(pre_grad, gate_up, pick, gates)


def body(
    grad_out,
    routes,
    gate_probs,
    saved_pre,
    down_weight,
    gate_up_weight,
    queries,
    keys_values,
    attn_grad,
    attn_out,
):
    experts = lax.axis_size("exp")
    contexts = lax.axis_size("ctx")
    tok_rows = grad_out.shape[1]
    width = grad_out.shape[2]
    filled = saved_pre.shape[2] // experts
    capacity = -(-filled // 16) * 16
    hidden = down_weight.shape[1]
    chips = contexts // 2

    route_rows = routes[0]
    one_hot = (
        route_rows.reshape(-1)[:, None] == jnp.arange(experts, dtype=jnp.int32)[None, :]
    ).astype(jnp.int32)
    earlier = jnp.cumsum(one_hot, axis=0) - one_hot
    positions = jnp.sum(earlier * one_hot, axis=-1)
    slot_keys = route_rows[:, 0] * capacity + positions
    slots = experts * capacity

    kv_local = keys_values[0]
    kv_width = kv_local.shape[1]
    extra = jnp.broadcast_to(
        jnp.pad(slot_keys.astype(jnp.bfloat16), (0, kv_width - tok_rows))[None], (16, kv_width)
    )
    kv_wide = jnp.concatenate([kv_local, extra], axis=0)

    dispatch = (jnp.arange(slots, dtype=jnp.int32)[:, None] == slot_keys[None, :]).astype(
        jnp.bfloat16
    )
    send_rows = jnp.dot(dispatch, grad_out[0], preferred_element_type=jnp.float32).astype(
        jnp.bfloat16
    )
    query_grad, kv_grad, down_grad, block_extra = gather_and_attend(
        kv_wide,
        down_weight[0],
        send_rows.reshape(experts, capacity, width),
        queries[0],
        attn_grad[0],
        attn_out[0],
        chips,
    )
    block_keys = block_extra[:, 0, :tok_rows].astype(jnp.int32)

    pre_acts = saved_pre[0, 0]
    if capacity != filled:
        pre_acts = pre_acts.reshape(experts, filled, 2 * hidden)
        pre_acts = jnp.pad(pre_acts, ((0, 0), (0, capacity - filled), (0, 0)))
        pre_acts = pre_acts.reshape(slots, 2 * hidden)
    gate_pre = pre_acts[:, :hidden].astype(jnp.float32)
    up_pre = pre_acts[:, hidden:].astype(jnp.float32)
    sigma = jax.nn.sigmoid(gate_pre)
    swish = gate_pre * sigma
    slot_prob = jnp.sum(down_grad * swish * up_pre, axis=-1).astype(jnp.bfloat16)
    gate_part = down_grad * up_pre * sigma * (1.0 + gate_pre * (1.0 - sigma))
    up_part = down_grad * swish
    pre_grad = jnp.concatenate([gate_part, up_part], axis=-1).astype(jnp.bfloat16)

    back_prob = lax.all_to_all(
        slot_prob.reshape(experts, capacity), "exp", split_axis=0, concat_axis=0, tiled=True
    ).reshape(slots)
    pick = (block_keys[:, :, None] == jnp.arange(slots, dtype=jnp.int32)).astype(jnp.bfloat16)
    moe_input_grad = expert_return(
        pre_grad, gate_up_weight[0], pick, gate_probs[0], chips, experts
    )[None]
    own_slots = slot_keys[:, None] == jnp.arange(slots, dtype=jnp.int32)
    prob_grad = jnp.sum(
        jnp.where(own_slots, back_prob.astype(jnp.float32), 0.0), axis=1
    ).astype(jnp.bfloat16)[None, :, None]
    return (moe_input_grad, prob_grad, query_grad[None], kv_grad[None])


def solution(mesh):
    tok = P("exp", "ctx", None)
    placed = (
        tok,
        tok,
        tok,
        P("ctx", "exp", None, None),
        P("exp", None, "ctx"),
        tok,
        tok,
        tok,
        tok,
        tok,
    )
    return jax.shard_map(
        body,
        mesh=mesh,
        in_specs=placed,
        out_specs=(tok, tok, tok, tok),
        check_vma=False,
    )
```

```python
import functools

import jax
import jax.numpy as jnp
from jax import lax
from jax.experimental import pallas as pl
from jax.experimental.pallas import tpu as pltpu
from jax.sharding import PartitionSpec as P

KEY_VALUE_HEADS = 2
HEAD_SIZE = 128
LOG2E = 1.4426950408889634
PARTS = 2
NT = (((1,), (1,)), ((), ()))


MESH = pl.DeviceIdType.MESH


def gather_kernel(
    chips,
    experts,
    routes_ref,
    kv_ref,
    down_ref,
    token_ref,
    acts_ref,
    q_ref,
    g_ref,
    o_ref,
    dq_ref,
    kv_grad_ref,
    pre_ref,
    prob_ref,
    pick_ref,
    rows_ref,
    hidden_ref,
    kv_buf,
    down_buf,
    row_buf,
    kv_all,
    terms,
    keys_t,
    bias,
    scores,
    low_grads,
    pair_terms,
    leaving,
    landed,
    kv_up,
    kv_down,
    kv_in,
    kv_swap_out,
    kv_swap_in,
    w_up,
    w_down,
    w_in,
    w_swap_out,
    w_swap_in,
    row_out,
    row_in,
    pair_out,
    pair_in,
    term_out,
    term_in,
):
    me = lax.axis_index("ctx")
    mine = lax.axis_index("exp")
    z = lax.div(me, 2)
    core = lax.rem(me, 2)
    partner = 2 * z + 1 - core
    tok_rows, width = q_ref.shape
    seq_len = kv_all.shape[0]
    hd = HEAD_SIZE
    has_up = z + 1 < chips
    has_down = z > 0

    barrier = pltpu.get_barrier_semaphore()
    for d in range(1, chips):
        chip = lax.rem(z + d, chips)
        pl.semaphore_signal(
            barrier, inc=1, device_id={"ctx": 2 * chip + core}, device_id_type=MESH
        )
    for d in range(1, experts):
        pl.semaphore_signal(
            barrier, inc=1, device_id={"exp": lax.rem(mine + d, experts)}, device_id_type=MESH
        )
    pl.semaphore_signal(barrier, inc=1, device_id={"ctx": partner}, device_id_type=MESH)
    capacity = rows_ref.shape[1]
    slots = experts * capacity
    routes = routes_ref[...]
    at = lax.broadcasted_iota(jnp.int32, (-(-experts // 16) * 16, tok_rows), 0)
    named = jnp.where(at == routes, 1.0, 0.0).astype(jnp.float32)
    row = lax.broadcasted_iota(jnp.int32, (tok_rows, tok_rows), 0)
    col = lax.broadcasted_iota(jnp.int32, (tok_rows, tok_rows), 1)
    before = jnp.where(row < col, 1.0, 0.0).astype(jnp.bfloat16)
    earlier = jnp.dot(named.astype(jnp.bfloat16), before, preferred_element_type=jnp.float32)
    place = jnp.sum(earlier * named, axis=0, keepdims=True)
    slot_keys = routes.astype(jnp.float32) * capacity + place

    def one_hot(keys):
        at = lax.broadcasted_iota(jnp.int32, (slots, tok_rows), 0).astype(jnp.float32)
        return jnp.where(at == keys, 1.0, 0.0).astype(jnp.float32)

    extra = kv_buf.shape[2] - tok_rows
    kv_buf[z, core, :tok_rows, :] = kv_ref[...]
    kv_buf[z, core, tok_rows:, :] = jnp.zeros((extra, kv_ref.shape[1]), kv_buf.dtype)
    kv_buf[z, core, tok_rows:, :tok_rows] = jnp.broadcast_to(slot_keys, (extra, tok_rows)).astype(
        kv_buf.dtype
    )
    down_buf[z, core] = down_ref[...]
    pl.semaphore_wait(barrier, chips + experts - 1)

    def remote(src, dst, send, recv, device):
        return pltpu.make_async_remote_copy(
            src_ref=src,
            dst_ref=dst,
            send_sem=send,
            recv_sem=recv,
            device_id=device,
            device_id_type=MESH,
        )

    class Line:
        def __init__(self, buf, parts, up, down, arrived, swap_out, swap_in):
            self.buf, self.sems = buf, (up, down, arrived, swap_out, swap_in)
            self.parts, self.rows = parts, buf.shape[2] // parts

        def piece(self, b, p, side):
            return self.buf.at[b, side, pl.ds(p * self.rows, self.rows), :]

        def up(self, b, p):
            ref = self.piece(b, p, core)
            return remote(ref, ref, self.sems[0].at[b, p], self.sems[2].at[b, p], {"ctx": me + 2})

        def down(self, b, p):
            ref = self.piece(b, p, core)
            return remote(ref, ref, self.sems[1].at[b, p], self.sems[2].at[b, p], {"ctx": me - 2})

        def swap(self, b, p, side):
            ref = self.piece(b, p, side)
            return remote(ref, ref, self.sems[3].at[b, p], self.sems[4].at[b, p], {"ctx": partner})

        def begin(self):
            for p in range(self.parts):

                @pl.when(has_up)
                def _():
                    self.up(z, p).start()

                @pl.when(has_down)
                def _():
                    self.down(z, p).start()

            for p in range(self.parts):
                self.swap(z, p, core).start()

        def relay(self, i, p, on=True):
            lo = z - i
            hi = z + i

            @pl.when((lo >= 0) & on)
            def _():
                self.up(lo, p).wait_recv()

                @pl.when(has_up)
                def _():
                    self.up(lo, p).start()

                self.swap(lo, p, core).start()

            @pl.when((hi < chips) & on)
            def _():
                self.down(hi, p).wait_recv()

                @pl.when(has_down)
                def _():
                    self.down(hi, p).start()

                self.swap(hi, p, core).start()

        def finish(self):
            for b in range(chips):
                for p in range(self.parts):

                    @pl.when(has_up & (z >= b))
                    def _():
                        self.up(b, p).wait_send()

                    @pl.when(has_down & (z <= b))
                    def _():
                        self.down(b, p).wait_send()

                    self.swap(b, p, core).wait_send()

    kv_line = Line(kv_buf, 1, kv_up, kv_down, kv_in, kv_swap_out, kv_swap_in)
    w_line = Line(down_buf, PARTS, w_up, w_down, w_in, w_swap_out, w_swap_in)

    def cross(to, slot):
        return remote(
            rows_ref.at[to], row_buf.at[slot], row_out.at[to], row_in.at[slot], {"exp": to}
        )

    kv_line.begin()
    w_line.begin()
    dispatch = one_hot(slot_keys).astype(jnp.bfloat16)
    wide = 512
    for t in range(width // wide):
        cols = pl.ds(t * wide, wide)
        rows_ref[:, :, cols] = (
            jnp.dot(dispatch, token_ref[:, cols], preferred_element_type=jnp.float32)
            .astype(rows_ref.dtype)
            .reshape(experts, capacity, wide)
        )
    for d in range(1, experts):
        cross(lax.rem(mine + d, experts), mine).start()
    row_buf[mine] = rows_ref[mine]

    terms[...] = jnp.zeros_like(terms)
    key_pos = lax.broadcasted_iota(jnp.int32, bias.shape, 0)
    row_pos = me * tok_rows + lax.rem(lax.broadcasted_iota(jnp.int32, bias.shape, 1), tok_rows)
    bias[...] = jnp.where(key_pos <= row_pos, 0.0, -1e30).astype(jnp.float32)
    for i in range(1, chips):
        kv_line.relay(i, 0)
    for b in range(chips):
        kv_line.swap(b, 0, 1 - core).wait_recv()
        for side in range(2):
            kv_all[pl.ds((2 * b + side) * tok_rows, tok_rows), :] = kv_buf[b, side, :tok_rows, :]
        keys = kv_buf[b, core, tok_rows:, :tok_rows].astype(jnp.float32)
        pick_ref[b] = one_hot(keys[:1]).T.astype(pick_ref.dtype)
    for head in range(KEY_VALUE_HEADS):
        keys = kv_all[:, 2 * hd * head : 2 * hd * head + hd]
        keys_t[head] = keys.astype(jnp.float32).T.astype(jnp.bfloat16)

    scale = hd**-0.5
    chunk = 256
    chunks = [pl.ds(i * chunk, chunk) for i in range(seq_len // chunk)]
    pairs = scores.shape[0]
    step = 2 * pairs * hd
    units = width // step

    def unit(u, carry):
        for when, i, p in ((0, 1, 0), (2, 1, 1), (5, 2, 0), (7, 2, 1)):
            if i < chips:

                @pl.when(u == when)
                def _():
                    w_line.relay(i, p)

        head = lax.div(u, units // KEY_VALUE_HEADS)
        key_cols = pl.ds(pl.multiple_of(head * 2 * hd, hd), hd)
        val_cols = pl.ds(pl.multiple_of(head * 2 * hd + hd, hd), hd)
        for pair in range(pairs):
            cols = [
                pl.ds(pl.multiple_of(u * step + (2 * pair + i) * hd, hd), hd) for i in range(2)
            ]
            q2 = jnp.concatenate([q_ref[:, col] for col in cols], axis=0)
            g2 = jnp.concatenate([g_ref[:, col] for col in cols], axis=0)
            o2 = jnp.concatenate([o_ref[:, col] for col in cols], axis=0)
            prod = g2.astype(jnp.float32) * o2.astype(jnp.float32)
            delta = jnp.sum(prod.T, axis=0, keepdims=True)
            top = jnp.full((1, 2 * tok_rows), -jnp.inf, jnp.float32)
            for part in chunks:
                s = lax.dot_general(
                    kv_all[part, key_cols], q2, NT, preferred_element_type=jnp.float32
                )
                s = s + bias[part, :]
                scores[pair, part, :] = s
                top = jnp.maximum(top, jnp.max(s, axis=0, keepdims=True))
            total = jnp.zeros((1, 2 * tok_rows), jnp.float32)
            for part in chunks:
                e = jnp.exp2((scores[pair, part, :] - top) * (scale * LOG2E))
                scores[pair, part, :] = e
                total = total + jnp.sum(e, axis=0, keepdims=True)
            inverse = 1.0 / total
            for part in chunks:
                p = scores[pair, part, :] * inverse
                terms[part, val_cols] += jnp.dot(
                    p.astype(jnp.bfloat16), g2, preferred_element_type=jnp.float32
                )
                dp = lax.dot_general(
                    kv_all[part, val_cols], g2, NT, preferred_element_type=jnp.float32
                )
                ds = (p * (dp - delta)).astype(jnp.bfloat16)
                low_grads[pair, part, :] = ds
                terms[part, key_cols] += (
                    jnp.dot(ds, q2, preferred_element_type=jnp.float32) * scale
                )
            dq = (
                jnp.dot(keys_t[head], low_grads[pair], preferred_element_type=jnp.float32) * scale
            ).T
            for i in range(2):
                dq_ref[:, cols[i]] = dq[i * tok_rows : (i + 1) * tok_rows].astype(dq_ref.dtype)
        return carry

    lax.fori_loop(0, units, unit, 0)

    def rows_of(b, side):
        return pl.ds(pl.multiple_of((2 * b + side) * tok_rows, tok_rows), tok_rows)

    def pair_copy(b, side):
        return remote(
            terms.at[rows_of(b, side), :],
            pair_terms.at[b],
            pair_out.at[b],
            pair_in.at[b],
            {"ctx": partner},
        )

    def term_copy(b, slot):
        return remote(
            leaving.at[b],
            landed.at[slot],
            term_out.at[b],
            term_in.at[slot],
            {"ctx": 2 * b + core},
        )

    for b in range(chips):

        @pl.when(b <= z)
        def _():
            pair_copy(b, 1 - core).start()

    for d in range(1, experts):
        j = lax.rem(mine + d, experts)
        cross(j, j).wait_recv()
    hidden_ref[...] = jnp.zeros_like(hidden_ref)
    shard = down_ref.shape[1]
    hidden = hidden_ref.shape[1]
    piece = hidden // PARTS

    def hidden_part(i, p):
        w_line.relay(i, p, i >= 3)
        ahead = lax.rem(z + i, chips)
        behind = lax.rem(z - i + chips, chips)
        b = jnp.where(z < chips // 2, ahead, behind)
        w_line.swap(b, p, 1 - core).wait_recv()
        part = pl.ds(p * piece, piece)
        for side in range(2):
            cols = pl.ds(pl.multiple_of((2 * b + side) * shard, shard), shard)
            rows = row_buf[:, :, cols].reshape(slots, shard)
            hidden_ref[:, part] += lax.dot_general(
                rows, down_buf[b, side, part, :], NT, preferred_element_type=jnp.float32
            )

    def hidden_turn(i, carry):
        for p in range(PARTS):
            hidden_part(i, p)
        return carry

    lax.fori_loop(0, chips - 1, hidden_turn, 0)

    for b in range(chips):

        @pl.when(b <= z)
        def _():
            pair_copy(b, core).wait_recv()

        @pl.when(b < z)
        def _():
            leaving[b] = (terms[rows_of(b, core), :] + pair_terms[b]).astype(leaving.dtype)
            term_copy(b, z).start()

    prob = jnp.zeros((slots, 1), jnp.float32)
    tile = 128
    for p in range(PARTS):
        hidden_part(chips - 1, p)
        for t in range(p * piece, (p + 1) * piece, tile):
            grad = hidden_ref[:, t : t + tile]
            gate_pre = acts_ref[:, t : t + tile].astype(jnp.float32)
            up_pre = acts_ref[:, hidden + t : hidden + t + tile].astype(jnp.float32)
            sigma = jax.nn.sigmoid(gate_pre)
            swish = gate_pre * sigma
            up_part = grad * swish
            prob = prob + jnp.sum(up_part * up_pre, axis=-1, keepdims=True)
            gate_part = grad * up_pre * sigma * (1.0 + gate_pre * (1.0 - sigma))
            pre_ref[:, t : t + tile] = gate_part.astype(pre_ref.dtype)
            pre_ref[:, hidden + t : hidden + t + tile] = up_part.astype(pre_ref.dtype)
    prob_ref[...] = (
        jnp.broadcast_to(prob, (slots, prob_ref.shape[2]))
        .astype(prob_ref.dtype)
        .reshape(prob_ref.shape)
    )

    landed_sum = terms[rows_of(z, core), :] + pair_terms[z]
    kv_sum = pair_terms.at[z]
    kv_sum[...] = landed_sum
    for b in range(chips):

        @pl.when(b > z)
        def _():
            term_copy(b, b).wait_recv()
            kv_sum[...] += landed[b].astype(jnp.float32)

    kv_grad_ref[...] = kv_sum[...].astype(kv_grad_ref.dtype)

    kv_line.finish()
    w_line.finish()
    for d in range(1, experts):
        cross(lax.rem(mine + d, experts), mine).wait_send()
    for b in range(chips):

        @pl.when(b <= z)
        def _():
            pair_copy(b, 1 - core).wait_send()

        @pl.when(b < z)
        def _():
            term_copy(b, z).wait_send()


def gather_and_attend(routes, kv_local, down, tokens, acts, q, g, o, chips, experts):
    tok_rows, width = q.shape
    kv_width = kv_local.shape[1]
    seq_len = 2 * chips * tok_rows
    hidden, shard = down.shape
    slots = acts.shape[0]
    capacity = slots // experts
    hd = HEAD_SIZE
    pairs = 2
    vmem = pl.BlockSpec(memory_space=pltpu.VMEM)
    low, full = jnp.bfloat16, jnp.float32
    dma = pltpu.SemaphoreType.DMA
    per_chip = dma((chips,))
    return pl.pallas_call(
        functools.partial(gather_kernel, chips, experts),
        in_specs=[vmem] * 8,
        out_specs=[vmem] * 5,
        out_shape=[
            jax.ShapeDtypeStruct((tok_rows, width), low),
            jax.ShapeDtypeStruct((tok_rows, kv_width), low),
            jax.ShapeDtypeStruct((slots, 2 * hidden), low),
            jax.ShapeDtypeStruct((experts, capacity, 128), low),
            jax.ShapeDtypeStruct((chips, tok_rows, slots), low),
        ],
        scratch_shapes=[
            pltpu.VMEM((experts, capacity, width), low),
            pltpu.VMEM((slots, hidden), full),
            pltpu.VMEM((chips, 2, tok_rows + 16, kv_width), low),
            pltpu.VMEM((chips, 2, hidden, shard), low),
            pltpu.VMEM((experts, capacity, width), low),
            pltpu.VMEM((seq_len, kv_width), low),
            pltpu.VMEM((seq_len, kv_width), full),
            pltpu.VMEM((KEY_VALUE_HEADS, hd, seq_len), low),
            pltpu.VMEM((seq_len, 2 * tok_rows), full),
            pltpu.VMEM((pairs, seq_len, 2 * tok_rows), full),
            pltpu.VMEM((pairs, seq_len, 2 * tok_rows), low),
            pltpu.VMEM((chips, tok_rows, kv_width), full),
            pltpu.VMEM((chips, tok_rows, kv_width), low),
            pltpu.VMEM((chips, tok_rows, kv_width), low),
        ]
        + [dma((chips, 1))] * 5
        + [dma((chips, PARTS))] * 5
        + [dma((experts,))] * 2
        + [per_chip] * 4,
        compiler_params=pltpu.CompilerParams(
            collective_id=1, has_side_effects=True, vmem_limit_bytes=54 * 1024 * 1024
        ),
        cost_estimate=pl.CostEstimate(
            flops=10 * tok_rows * seq_len * width,
            bytes_accessed=8 * tok_rows * width,
            transcendentals=tok_rows * seq_len * width // hd,
        ),
    )(routes, kv_local, down, tokens, acts, q, g, o)


def return_kernel(
    chips,
    experts,
    pre_ref,
    gu_ref,
    pick_ref,
    gate_ref,
    prob_ref,
    out_ref,
    token_prob_ref,
    prob_buf,
    pre_buf,
    gu_buf,
    sent,
    came,
    leaving,
    landed,
    pair_sems,
    prob_out,
    prob_in,
    up_sems,
    down_sems,
    pre_sems,
    cross_out,
    cross_in,
    back_out,
    back_in,
):
    me = lax.axis_index("ctx")
    mine = lax.axis_index("exp")
    z = lax.div(me, 2)
    core = lax.rem(me, 2)
    shard = gu_ref.shape[0]
    columns = 2 * shard
    tile = min(shard, 256)

    barrier = pltpu.get_barrier_semaphore()
    for d in range(1, chips):
        chip = lax.rem(z + d, chips)
        pl.semaphore_signal(
            barrier, inc=1, device_id={"ctx": 2 * chip + core}, device_id_type=MESH
        )
    for d in range(1, experts):
        pl.semaphore_signal(
            barrier, inc=1, device_id={"exp": lax.rem(mine + d, experts)}, device_id_type=MESH
        )
    other = 2 * z + 1 - core
    pl.semaphore_signal(barrier, inc=1, device_id={"ctx": other}, device_id_type=MESH)
    pre_buf[z] = pre_ref[...]
    pl.semaphore_wait(barrier, chips + experts - 1)

    def remote(src, dst, send, recv, device):
        return pltpu.make_async_remote_copy(
            src_ref=src,
            dst_ref=dst,
            send_sem=send,
            recv_sem=recv,
            device_id=device,
            device_id_type=MESH,
        )

    def up(b):
        return remote(
            pre_buf.at[b], pre_buf.at[b], up_sems.at[b], pre_sems.at[b], {"ctx": me + 2}
        )

    def down(b):
        return remote(
            pre_buf.at[b], pre_buf.at[b], down_sems.at[b], pre_sems.at[b], {"ctx": me - 2}
        )

    def cross(b, to, slot):
        return remote(
            sent.at[b, to], came.at[b, slot], cross_out.at[b, to], cross_in.at[b, slot], {"exp": to}
        )

    def back(b, slot):
        return remote(
            leaving.at[b],
            landed.at[slot],
            back_out.at[b],
            back_in.at[slot],
            {"ctx": 2 * b + core},
        )

    swap = remote(
        gu_ref, gu_buf.at[core], pair_sems.at[0], pair_sems.at[1], {"ctx": other}
    )
    has_up = z + 1 < chips
    has_down = z > 0

    @pl.when(has_up)
    def _():
        up(z).start()

    @pl.when(has_down)
    def _():
        down(z).start()

    def prob_copy(to, slot):
        return remote(
            prob_ref.at[to], prob_buf.at[slot], prob_out.at[to], prob_in.at[slot], {"exp": to}
        )

    swap.start()
    keep = pltpu.make_async_copy(gu_ref, gu_buf.at[core], pair_sems.at[2])
    keep.start()
    for d in range(1, experts):
        prob_copy(lax.rem(mine + d, experts), mine).start()
    prob_buf[mine] = prob_ref[mine]
    keep.wait()
    swap.wait_recv()

    def block_of(i):
        ahead = lax.rem(z + i, chips)
        behind = lax.rem(z - i + chips, chips)
        return jnp.where(z < chips // 2, ahead, behind)

    def combine(b):
        for d in range(1, experts):
            j = lax.rem(mine + d, experts)
            cross(b, j, j).wait_recv()
        slots = pick_ref.shape[2]
        for t in range(columns // tile):
            cols = pl.ds(t * tile, tile)
            rows = came[b, :, :, cols].reshape(slots, tile)
            leaving[b, :, cols] = jnp.dot(
                pick_ref[b], rows, preferred_element_type=jnp.float32
            ).astype(leaving.dtype)

        @pl.when(b != z)
        def _():
            back(b, z).start()

        @pl.when(b == z)
        def _():
            landed[z] = leaving[b]

    def turn(i, carry):
        lo = z - i
        hi = z + i

        @pl.when((i > 0) & (lo >= 0))
        def _():
            up(lo).wait_recv()

            @pl.when(has_up)
            def _():
                up(lo).start()

        @pl.when((i > 0) & (hi < chips))
        def _():
            down(hi).wait_recv()

            @pl.when(has_down)
            def _():
                down(hi).start()

        b = block_of(i)
        for half in range(2):
            for t in range(shard // tile):
                weights = gu_buf[half, pl.ds(t * tile, tile), :]
                grads = lax.dot_general(
                    pre_buf[b], weights, NT, preferred_element_type=jnp.float32
                )
                cols = pl.ds(half * shard + t * tile, tile)
                sent[b, :, :, cols] = grads.astype(sent.dtype).reshape(experts, -1, tile)
        for d in range(1, experts):
            cross(b, lax.rem(mine + d, experts), mine).start()
        came[b, mine] = sent[b, mine]

        @pl.when(i > 0)
        def _():
            combine(block_of(i - 1))

        return carry

    lax.fori_loop(0, chips, turn, 0)
    combine(block_of(chips - 1))
    for b in range(chips):

        @pl.when(z != b)
        def _():
            back(b, b).wait_recv()

        out_ref[:, pl.ds(b * columns, columns)] = (
            gate_ref[...] * landed[b].astype(jnp.float32)
        ).astype(out_ref.dtype)

    for d in range(1, experts):
        j = lax.rem(mine + d, experts)
        prob_copy(j, j).wait_recv()
    lanes = prob_ref.shape[2]
    token_prob_ref[...] = jnp.dot(
        pick_ref[z],
        prob_buf[...].reshape(pick_ref.shape[2], lanes),
        preferred_element_type=jnp.float32,
    ).astype(token_prob_ref.dtype)

    swap.wait_send()
    for d in range(1, experts):
        prob_copy(lax.rem(mine + d, experts), mine).wait_send()
    for b in range(chips):

        @pl.when(has_up & (z >= b))
        def _():
            up(b).wait_send()

        @pl.when(has_down & (z <= b))
        def _():
            down(b).wait_send()

        @pl.when(z != b)
        def _():
            back(b, z).wait_send()

        for d in range(1, experts):
            cross(b, lax.rem(mine + d, experts), mine).wait_send()


def expert_return(pre_grad, gate_up, pick, gates, prob, chips, experts):
    slots, pre_width = pre_grad.shape
    capacity = slots // experts
    shard = gate_up.shape[0]
    tok_rows = gates.shape[0]
    columns = 2 * shard
    vmem = pl.BlockSpec(memory_space=pltpu.VMEM)
    low = jnp.bfloat16
    dma = pltpu.SemaphoreType.DMA
    return pl.pallas_call(
        functools.partial(return_kernel, chips, experts),
        in_specs=[vmem, pl.BlockSpec(memory_space=pl.ANY), vmem, vmem, vmem],
        out_specs=[vmem, vmem],
        out_shape=[
            jax.ShapeDtypeStruct((tok_rows, chips * columns), low),
            jax.ShapeDtypeStruct((tok_rows, prob.shape[2]), low),
        ],
        scratch_shapes=[
            pltpu.VMEM(prob.shape, low),
            pltpu.VMEM((chips, slots, pre_width), low),
            pltpu.VMEM((2, shard, pre_width), low),
            pltpu.VMEM((chips, experts, capacity, columns), low),
            pltpu.VMEM((chips, experts, capacity, columns), low),
            pltpu.VMEM((chips, tok_rows, columns), low),
            pltpu.VMEM((chips, tok_rows, columns), low),
            dma((3,)),
            dma((experts,)),
            dma((experts,)),
            dma((chips,)),
            dma((chips,)),
            dma((chips,)),
            dma((chips, experts)),
            dma((chips, experts)),
            dma((chips,)),
            dma((chips,)),
        ],
        compiler_params=pltpu.CompilerParams(
            collective_id=0, has_side_effects=True, vmem_limit_bytes=40 * 1024 * 1024
        ),
        cost_estimate=pl.CostEstimate(
            flops=2 * chips * slots * pre_width * columns,
            bytes_accessed=4 * (slots * pre_width + shard * pre_width),
            transcendentals=0,
        ),
    )(pre_grad, gate_up, pick, gates, prob)


def body(
    grad_out,
    routes,
    gate_probs,
    saved_pre,
    down_weight,
    gate_up_weight,
    queries,
    keys_values,
    attn_grad,
    attn_out,
):
    experts = lax.axis_size("exp")
    contexts = lax.axis_size("ctx")
    tok_rows = grad_out.shape[1]
    filled = saved_pre.shape[2] // experts
    capacity = -(-filled // 16) * 16
    hidden = down_weight.shape[1]
    chips = contexts // 2

    pre_acts = saved_pre[0, 0]
    if capacity != filled:
        pre_acts = pre_acts.reshape(experts, filled, 2 * hidden)
        pre_acts = jnp.pad(pre_acts, ((0, 0), (0, capacity - filled), (0, 0)))
        pre_acts = pre_acts.reshape(experts * capacity, 2 * hidden)
    query_grad, kv_grad, pre_grad, prob, pick = gather_and_attend(
        routes.reshape(1, tok_rows),
        keys_values[0],
        down_weight[0],
        grad_out[0],
        pre_acts,
        queries[0],
        attn_grad[0],
        attn_out[0],
        chips,
        experts,
    )
    moe_input_grad, token_prob = expert_return(
        pre_grad, gate_up_weight[0], pick, gate_probs[0], prob, chips, experts
    )
    prob_grad = token_prob[:, :1][None]
    return (moe_input_grad[None], prob_grad, query_grad[None], kv_grad[None])


def solution(mesh):
    tok = P("exp", "ctx", None)
    placed = (
        tok,
        tok,
        tok,
        P("ctx", "exp", None, None),
        P("exp", None, "ctx"),
        tok,
        tok,
        tok,
        tok,
        tok,
    )
    return jax.shard_map(
        body,
        mesh=mesh,
        in_specs=placed,
        out_specs=(tok, tok, tok, tok),
        check_vma=False,
    )
```

```python
import functools

import jax
import jax.numpy as jnp
from jax import lax
from jax.experimental import pallas as pl
from jax.experimental.pallas import tpu as pltpu
from jax.sharding import PartitionSpec as P

KEY_VALUE_HEADS = 2
HEAD_SIZE = 128
LOG2E = 1.4426950408889634
PARTS = 2
NT = (((1,), (1,)), ((), ()))


MESH = pl.DeviceIdType.MESH


def return_parts(
    chips,
    experts,
    gu_ref,
    pick_ref,
    gate_ref,
    prob_ref,
    out_ref,
    token_prob_ref,
    prob_buf,
    pre_buf,
    gu_buf,
    sent,
    came,
    leaving,
    landed,
    pair_sems,
    prob_out,
    prob_in,
    up_sems,
    down_sems,
    pre_sems,
    cross_out,
    cross_in,
    back_out,
    back_in,
):
    me = lax.axis_index("ctx")
    mine = lax.axis_index("exp")
    z = lax.div(me, 2)
    core = lax.rem(me, 2)
    shard = gu_ref.shape[0]
    columns = 2 * shard
    tile = min(shard, 256)

    other = 2 * z + 1 - core

    def remote(src, dst, send, recv, device):
        return pltpu.make_async_remote_copy(
            src_ref=src,
            dst_ref=dst,
            send_sem=send,
            recv_sem=recv,
            device_id=device,
            device_id_type=MESH,
        )

    def up(b):
        return remote(
            pre_buf.at[b], pre_buf.at[b], up_sems.at[b], pre_sems.at[b], {"ctx": me + 2}
        )

    def down(b):
        return remote(
            pre_buf.at[b], pre_buf.at[b], down_sems.at[b], pre_sems.at[b], {"ctx": me - 2}
        )

    def cross(b, to, slot):
        return remote(
            sent.at[b, to], came.at[b, slot], cross_out.at[b, to], cross_in.at[b, slot], {"exp": to}
        )

    def back(b, slot):
        return remote(
            leaving.at[b],
            landed.at[slot],
            back_out.at[b],
            back_in.at[slot],
            {"ctx": 2 * b + core},
        )

    swap = remote(
        gu_ref, gu_buf.at[core], pair_sems.at[0], pair_sems.at[1], {"ctx": other}
    )
    has_up = z + 1 < chips
    has_down = z > 0

    def prob_copy(to, slot):
        return remote(
            prob_ref.at[to], prob_buf.at[slot], prob_out.at[to], prob_in.at[slot], {"exp": to}
        )

    def block_of(i):
        ahead = lax.rem(z + i, chips)
        behind = lax.rem(z - i + chips, chips)
        return jnp.where(z < chips // 2, ahead, behind)

    def combine(b):
        for d in range(1, experts):
            j = lax.rem(mine + d, experts)
            cross(b, j, j).wait_recv()
        slots = pick_ref.shape[2]
        for t in range(columns // tile):
            cols = pl.ds(t * tile, tile)
            rows = came[b, :, :, cols].reshape(slots, tile)
            leaving[b, :, cols] = jnp.dot(
                pick_ref[b], rows, preferred_element_type=jnp.float32
            ).astype(leaving.dtype)

        @pl.when(b != z)
        def _():
            back(b, z).start()

        @pl.when(b == z)
        def _():
            landed[z] = leaving[b]

    def turn(i, carry):
        lo = z - i
        hi = z + i

        @pl.when((i > 0) & (lo >= 0))
        def _():
            up(lo).wait_recv()

            @pl.when(has_up)
            def _():
                up(lo).start()

        @pl.when((i > 0) & (hi < chips))
        def _():
            down(hi).wait_recv()

            @pl.when(has_down)
            def _():
                down(hi).start()

        b = block_of(i)
        for half in range(2):
            for t in range(shard // tile):
                weights = gu_buf[half, pl.ds(t * tile, tile), :]
                grads = lax.dot_general(
                    pre_buf[b], weights, NT, preferred_element_type=jnp.float32
                )
                cols = pl.ds(half * shard + t * tile, tile)
                sent[b, :, :, cols] = grads.astype(sent.dtype).reshape(experts, -1, tile)
        for d in range(1, experts):
            cross(b, lax.rem(mine + d, experts), mine).start()
        came[b, mine] = sent[b, mine]

        @pl.when(i > 0)
        def _():
            combine(block_of(i - 1))

        return carry

    keep = pltpu.make_async_copy(gu_ref, gu_buf.at[core], pair_sems.at[2])

    def early():
        swap.start()
        keep.start()

    def run():
        @pl.when(has_up)
        def _():
            up(z).start()

        @pl.when(has_down)
        def _():
            down(z).start()

        for d in range(1, experts):
            prob_copy(lax.rem(mine + d, experts), mine).start()
        prob_buf[mine] = prob_ref[mine]
        keep.wait()
        swap.wait_recv()

        lax.fori_loop(0, chips, turn, 0)
        combine(block_of(chips - 1))
        for b in range(chips):

            @pl.when(z != b)
            def _():
                back(b, b).wait_recv()

            out_ref[:, pl.ds(b * columns, columns)] = (
                gate_ref[...] * landed[b].astype(jnp.float32)
            ).astype(out_ref.dtype)

        for d in range(1, experts):
            j = lax.rem(mine + d, experts)
            prob_copy(j, j).wait_recv()
        lanes = prob_ref.shape[2]
        token_prob_ref[...] = jnp.dot(
            pick_ref[z],
            prob_buf[...].reshape(pick_ref.shape[2], lanes),
            preferred_element_type=jnp.float32,
        ).astype(token_prob_ref.dtype)

        swap.wait_send()
        for d in range(1, experts):
            prob_copy(lax.rem(mine + d, experts), mine).wait_send()
        for b in range(chips):

            @pl.when(has_up & (z >= b))
            def _():
                up(b).wait_send()

            @pl.when(has_down & (z <= b))
            def _():
                down(b).wait_send()

            @pl.when(z != b)
            def _():
                back(b, z).wait_send()

            for d in range(1, experts):
                cross(b, lax.rem(mine + d, experts), mine).wait_send()

    return early, run


def layer_kernel(
    chips,
    experts,
    routes_ref,
    kv_ref,
    down_ref,
    token_ref,
    acts_ref,
    q_ref,
    g_ref,
    o_ref,
    gate_ref,
    gu_ref,
    dq_ref,
    kv_grad_ref,
    out_ref,
    token_prob_ref,
    prob_ref,
    pick_ref,
    rows_ref,
    hidden_ref,
    kv_buf,
    down_buf,
    row_buf,
    kv_all,
    terms,
    keys_t,
    bias,
    scores,
    low_grads,
    pair_terms,
    leaving,
    landed,
    kv_up,
    kv_down,
    kv_in,
    kv_swap_out,
    kv_swap_in,
    w_up,
    w_down,
    w_in,
    w_swap_out,
    w_swap_in,
    row_out,
    row_in,
    pair_out,
    pair_in,
    term_out,
    term_in,
    prob_buf,
    pre_buf,
    *return_refs,
):
    me = lax.axis_index("ctx")
    mine = lax.axis_index("exp")
    z = lax.div(me, 2)
    core = lax.rem(me, 2)
    partner = 2 * z + 1 - core
    tok_rows, width = q_ref.shape
    seq_len = kv_all.shape[0]
    hd = HEAD_SIZE
    has_up = z + 1 < chips
    has_down = z > 0

    barrier = pltpu.get_barrier_semaphore()
    for d in range(1, chips):
        chip = lax.rem(z + d, chips)
        pl.semaphore_signal(
            barrier, inc=1, device_id={"ctx": 2 * chip + core}, device_id_type=MESH
        )
    for d in range(1, experts):
        pl.semaphore_signal(
            barrier, inc=1, device_id={"exp": lax.rem(mine + d, experts)}, device_id_type=MESH
        )
    pl.semaphore_signal(barrier, inc=1, device_id={"ctx": partner}, device_id_type=MESH)
    capacity = rows_ref.shape[1]
    slots = experts * capacity
    routes = routes_ref[...]
    at = lax.broadcasted_iota(jnp.int32, (-(-experts // 16) * 16, tok_rows), 0)
    named = jnp.where(at == routes, 1.0, 0.0).astype(jnp.float32)
    row = lax.broadcasted_iota(jnp.int32, (tok_rows, tok_rows), 0)
    col = lax.broadcasted_iota(jnp.int32, (tok_rows, tok_rows), 1)
    before = jnp.where(row < col, 1.0, 0.0).astype(jnp.bfloat16)
    earlier = jnp.dot(named.astype(jnp.bfloat16), before, preferred_element_type=jnp.float32)
    place = jnp.sum(earlier * named, axis=0, keepdims=True)
    slot_keys = routes.astype(jnp.float32) * capacity + place

    def one_hot(keys):
        at = lax.broadcasted_iota(jnp.int32, (slots, tok_rows), 0).astype(jnp.float32)
        return jnp.where(at == keys, 1.0, 0.0).astype(jnp.float32)

    extra = kv_buf.shape[2] - tok_rows
    kv_buf[z, core, :tok_rows, :] = kv_ref[...]
    kv_buf[z, core, tok_rows:, :] = jnp.zeros((extra, kv_ref.shape[1]), kv_buf.dtype)
    kv_buf[z, core, tok_rows:, :tok_rows] = jnp.broadcast_to(slot_keys, (extra, tok_rows)).astype(
        kv_buf.dtype
    )
    down_buf[z, core] = down_ref[...]
    pl.semaphore_wait(barrier, chips + experts - 1)

    def remote(src, dst, send, recv, device):
        return pltpu.make_async_remote_copy(
            src_ref=src,
            dst_ref=dst,
            send_sem=send,
            recv_sem=recv,
            device_id=device,
            device_id_type=MESH,
        )

    class Line:
        def __init__(self, buf, parts, up, down, arrived, swap_out, swap_in):
            self.buf, self.sems = buf, (up, down, arrived, swap_out, swap_in)
            self.parts, self.rows = parts, buf.shape[2] // parts

        def piece(self, b, p, side):
            return self.buf.at[b, side, pl.ds(p * self.rows, self.rows), :]

        def up(self, b, p):
            ref = self.piece(b, p, core)
            return remote(ref, ref, self.sems[0].at[b, p], self.sems[2].at[b, p], {"ctx": me + 2})

        def down(self, b, p):
            ref = self.piece(b, p, core)
            return remote(ref, ref, self.sems[1].at[b, p], self.sems[2].at[b, p], {"ctx": me - 2})

        def swap(self, b, p, side):
            ref = self.piece(b, p, side)
            return remote(ref, ref, self.sems[3].at[b, p], self.sems[4].at[b, p], {"ctx": partner})

        def begin(self):
            for p in range(self.parts):

                @pl.when(has_up)
                def _():
                    self.up(z, p).start()

                @pl.when(has_down)
                def _():
                    self.down(z, p).start()

            for p in range(self.parts):
                self.swap(z, p, core).start()

        def relay(self, i, p, on=True):
            lo = z - i
            hi = z + i

            @pl.when((lo >= 0) & on)
            def _():
                self.up(lo, p).wait_recv()

                @pl.when(has_up)
                def _():
                    self.up(lo, p).start()

                self.swap(lo, p, core).start()

            @pl.when((hi < chips) & on)
            def _():
                self.down(hi, p).wait_recv()

                @pl.when(has_down)
                def _():
                    self.down(hi, p).start()

                self.swap(hi, p, core).start()

        def finish(self):
            for b in range(chips):
                for p in range(self.parts):

                    @pl.when(has_up & (z >= b))
                    def _():
                        self.up(b, p).wait_send()

                    @pl.when(has_down & (z <= b))
                    def _():
                        self.down(b, p).wait_send()

                    self.swap(b, p, core).wait_send()

    kv_line = Line(kv_buf, 1, kv_up, kv_down, kv_in, kv_swap_out, kv_swap_in)
    w_line = Line(down_buf, PARTS, w_up, w_down, w_in, w_swap_out, w_swap_in)

    def cross(to, slot):
        return remote(
            rows_ref.at[to], row_buf.at[slot], row_out.at[to], row_in.at[slot], {"exp": to}
        )

    early, run = return_parts(
        chips,
        experts,
        gu_ref,
        pick_ref,
        gate_ref,
        prob_ref,
        out_ref,
        token_prob_ref,
        prob_buf,
        pre_buf,
        *return_refs,
    )
    kv_line.begin()
    w_line.begin()
    early()
    dispatch = one_hot(slot_keys).astype(jnp.bfloat16)
    wide = 512
    for t in range(width // wide):
        cols = pl.ds(t * wide, wide)
        rows_ref[:, :, cols] = (
            jnp.dot(dispatch, token_ref[:, cols], preferred_element_type=jnp.float32)
            .astype(rows_ref.dtype)
            .reshape(experts, capacity, wide)
        )
    for d in range(1, experts):
        cross(lax.rem(mine + d, experts), mine).start()
    row_buf[mine] = rows_ref[mine]

    terms[...] = jnp.zeros_like(terms)
    key_pos = lax.broadcasted_iota(jnp.int32, bias.shape, 0)
    row_pos = me * tok_rows + lax.rem(lax.broadcasted_iota(jnp.int32, bias.shape, 1), tok_rows)
    bias[...] = jnp.where(key_pos <= row_pos, 0.0, -1e30).astype(jnp.float32)
    for i in range(1, chips):
        kv_line.relay(i, 0)
    for b in range(chips):
        kv_line.swap(b, 0, 1 - core).wait_recv()
        for side in range(2):
            kv_all[pl.ds((2 * b + side) * tok_rows, tok_rows), :] = kv_buf[b, side, :tok_rows, :]
        keys = kv_buf[b, core, tok_rows:, :tok_rows].astype(jnp.float32)
        pick_ref[b] = one_hot(keys[:1]).T.astype(pick_ref.dtype)
    for head in range(KEY_VALUE_HEADS):
        keys = kv_all[:, 2 * hd * head : 2 * hd * head + hd]
        keys_t[head] = keys.astype(jnp.float32).T.astype(jnp.bfloat16)

    scale = hd**-0.5
    chunk = 256
    chunks = [pl.ds(i * chunk, chunk) for i in range(seq_len // chunk)]
    pairs = scores.shape[0]
    step = 2 * pairs * hd
    units = width // step

    def unit(u, carry):
        for when, i, p in ((0, 1, 0), (2, 1, 1), (5, 2, 0), (7, 2, 1)):
            if i < chips:

                @pl.when(u == when)
                def _():
                    w_line.relay(i, p)

        head = lax.div(u, units // KEY_VALUE_HEADS)
        key_cols = pl.ds(pl.multiple_of(head * 2 * hd, hd), hd)
        val_cols = pl.ds(pl.multiple_of(head * 2 * hd + hd, hd), hd)
        for pair in range(pairs):
            cols = [
                pl.ds(pl.multiple_of(u * step + (2 * pair + i) * hd, hd), hd) for i in range(2)
            ]
            q2 = jnp.concatenate([q_ref[:, col] for col in cols], axis=0)
            g2 = jnp.concatenate([g_ref[:, col] for col in cols], axis=0)
            o2 = jnp.concatenate([o_ref[:, col] for col in cols], axis=0)
            prod = g2.astype(jnp.float32) * o2.astype(jnp.float32)
            delta = jnp.sum(prod.T, axis=0, keepdims=True)
            top = jnp.full((1, 2 * tok_rows), -jnp.inf, jnp.float32)
            for part in chunks:
                s = lax.dot_general(
                    kv_all[part, key_cols], q2, NT, preferred_element_type=jnp.float32
                )
                s = s + bias[part, :]
                scores[pair, part, :] = s
                top = jnp.maximum(top, jnp.max(s, axis=0, keepdims=True))
            total = jnp.zeros((1, 2 * tok_rows), jnp.float32)
            for part in chunks:
                e = jnp.exp2((scores[pair, part, :] - top) * (scale * LOG2E))
                scores[pair, part, :] = e
                total = total + jnp.sum(e, axis=0, keepdims=True)
            inverse = 1.0 / total
            for part in chunks:
                p = scores[pair, part, :] * inverse
                terms[part, val_cols] += jnp.dot(
                    p.astype(jnp.bfloat16), g2, preferred_element_type=jnp.float32
                )
                dp = lax.dot_general(
                    kv_all[part, val_cols], g2, NT, preferred_element_type=jnp.float32
                )
                ds = (p * (dp - delta)).astype(jnp.bfloat16)
                low_grads[pair, part, :] = ds
                terms[part, key_cols] += (
                    jnp.dot(ds, q2, preferred_element_type=jnp.float32) * scale
                )
            dq = (
                jnp.dot(keys_t[head], low_grads[pair], preferred_element_type=jnp.float32) * scale
            ).T
            for i in range(2):
                dq_ref[:, cols[i]] = dq[i * tok_rows : (i + 1) * tok_rows].astype(dq_ref.dtype)
        return carry

    lax.fori_loop(0, units, unit, 0)

    def rows_of(b, side):
        return pl.ds(pl.multiple_of((2 * b + side) * tok_rows, tok_rows), tok_rows)

    def pair_copy(b, side):
        return remote(
            terms.at[rows_of(b, side), :],
            pair_terms.at[b],
            pair_out.at[b],
            pair_in.at[b],
            {"ctx": partner},
        )

    def term_copy(b, slot):
        return remote(
            leaving.at[b],
            landed.at[slot],
            term_out.at[b],
            term_in.at[slot],
            {"ctx": 2 * b + core},
        )

    for b in range(chips):

        @pl.when(b <= z)
        def _():
            pair_copy(b, 1 - core).start()

    for d in range(1, experts):
        j = lax.rem(mine + d, experts)
        cross(j, j).wait_recv()
    hidden_ref[...] = jnp.zeros_like(hidden_ref)
    shard = down_ref.shape[1]
    hidden = hidden_ref.shape[1]
    piece = hidden // PARTS

    def hidden_part(i, p):
        w_line.relay(i, p, i >= 3)
        ahead = lax.rem(z + i, chips)
        behind = lax.rem(z - i + chips, chips)
        b = jnp.where(z < chips // 2, ahead, behind)
        w_line.swap(b, p, 1 - core).wait_recv()
        part = pl.ds(p * piece, piece)
        for side in range(2):
            cols = pl.ds(pl.multiple_of((2 * b + side) * shard, shard), shard)
            rows = row_buf[:, :, cols].reshape(slots, shard)
            hidden_ref[:, part] += lax.dot_general(
                rows, down_buf[b, side, part, :], NT, preferred_element_type=jnp.float32
            )

    def hidden_turn(i, carry):
        for p in range(PARTS):
            hidden_part(i, p)
        return carry

    lax.fori_loop(0, chips - 1, hidden_turn, 0)

    for b in range(chips):

        @pl.when(b <= z)
        def _():
            pair_copy(b, core).wait_recv()

        @pl.when(b < z)
        def _():
            leaving[b] = (terms[rows_of(b, core), :] + pair_terms[b]).astype(leaving.dtype)
            term_copy(b, z).start()

    prob = jnp.zeros((slots, 1), jnp.float32)
    tile = 128
    for p in range(PARTS):
        hidden_part(chips - 1, p)
        for t in range(p * piece, (p + 1) * piece, tile):
            grad = hidden_ref[:, t : t + tile]
            gate_pre = acts_ref[:, t : t + tile].astype(jnp.float32)
            up_pre = acts_ref[:, hidden + t : hidden + t + tile].astype(jnp.float32)
            sigma = jax.nn.sigmoid(gate_pre)
            swish = gate_pre * sigma
            up_part = grad * swish
            prob = prob + jnp.sum(up_part * up_pre, axis=-1, keepdims=True)
            gate_part = grad * up_pre * sigma * (1.0 + gate_pre * (1.0 - sigma))
            pre_buf[z, :, t : t + tile] = gate_part.astype(pre_buf.dtype)
            pre_buf[z, :, hidden + t : hidden + t + tile] = up_part.astype(pre_buf.dtype)
    prob_ref[...] = (
        jnp.broadcast_to(prob, (slots, prob_ref.shape[2]))
        .astype(prob_ref.dtype)
        .reshape(prob_ref.shape)
    )
    run()

    landed_sum = terms[rows_of(z, core), :] + pair_terms[z]
    kv_sum = pair_terms.at[z]
    kv_sum[...] = landed_sum
    for b in range(chips):

        @pl.when(b > z)
        def _():
            term_copy(b, b).wait_recv()
            kv_sum[...] += landed[b].astype(jnp.float32)

    kv_grad_ref[...] = kv_sum[...].astype(kv_grad_ref.dtype)

    kv_line.finish()
    w_line.finish()
    for d in range(1, experts):
        cross(lax.rem(mine + d, experts), mine).wait_send()
    for b in range(chips):

        @pl.when(b <= z)
        def _():
            pair_copy(b, 1 - core).wait_send()

        @pl.when(b < z)
        def _():
            term_copy(b, z).wait_send()


def layer_backward(
    routes, kv_local, down, tokens, acts, q, g, o, gates, gate_up, chips, experts
):
    tok_rows, width = q.shape
    kv_width = kv_local.shape[1]
    seq_len = 2 * chips * tok_rows
    hidden, shard = down.shape
    slots = acts.shape[0]
    capacity = slots // experts
    hd = HEAD_SIZE
    pairs = 2
    vmem = pl.BlockSpec(memory_space=pltpu.VMEM)
    low, full = jnp.bfloat16, jnp.float32
    dma = pltpu.SemaphoreType.DMA
    per_chip = dma((chips,))
    return pl.pallas_call(
        functools.partial(layer_kernel, chips, experts),
        in_specs=[vmem] * 9 + [pl.BlockSpec(memory_space=pl.ANY)],
        out_specs=[vmem] * 4,
        out_shape=[
            jax.ShapeDtypeStruct((tok_rows, width), low),
            jax.ShapeDtypeStruct((tok_rows, kv_width), low),
            jax.ShapeDtypeStruct((tok_rows, width), low),
            jax.ShapeDtypeStruct((tok_rows, 128), low),
        ],
        scratch_shapes=[
            pltpu.VMEM((experts, capacity, 128), low),
            pltpu.VMEM((chips, tok_rows, slots), low),
            pltpu.VMEM((experts, capacity, width), low),
            pltpu.VMEM((slots, hidden), full),
            pltpu.VMEM((chips, 2, tok_rows + 16, kv_width), low),
            pltpu.VMEM((chips, 2, hidden, shard), low),
            pltpu.VMEM((experts, capacity, width), low),
            pltpu.VMEM((seq_len, kv_width), low),
            pltpu.VMEM((seq_len, kv_width), full),
            pltpu.VMEM((KEY_VALUE_HEADS, hd, seq_len), low),
            pltpu.VMEM((seq_len, 2 * tok_rows), full),
            pltpu.VMEM((pairs, seq_len, 2 * tok_rows), full),
            pltpu.VMEM((pairs, seq_len, 2 * tok_rows), low),
            pltpu.VMEM((chips, tok_rows, kv_width), full),
            pltpu.VMEM((chips, tok_rows, kv_width), low),
            pltpu.VMEM((chips, tok_rows, kv_width), low),
        ]
        + [dma((chips, 1))] * 5
        + [dma((chips, PARTS))] * 5
        + [dma((experts,))] * 2
        + [per_chip] * 4
        + [
            pltpu.VMEM((experts, capacity, 128), low),
            pltpu.VMEM((chips, slots, 2 * hidden), low),
            pltpu.VMEM((2, shard, 2 * hidden), low),
            pltpu.VMEM((chips, experts, capacity, 2 * shard), low),
            pltpu.VMEM((chips, experts, capacity, 2 * shard), low),
            pltpu.VMEM((chips, tok_rows, 2 * shard), low),
            pltpu.VMEM((chips, tok_rows, 2 * shard), low),
            dma((3,)),
            dma((experts,)),
            dma((experts,)),
            per_chip,
            per_chip,
            per_chip,
            dma((chips, experts)),
            dma((chips, experts)),
            per_chip,
            per_chip,
        ],
        compiler_params=pltpu.CompilerParams(
            collective_id=0, has_side_effects=True, vmem_limit_bytes=60 * 1024 * 1024
        ),
        cost_estimate=pl.CostEstimate(
            flops=10 * tok_rows * seq_len * width,
            bytes_accessed=8 * tok_rows * width,
            transcendentals=tok_rows * seq_len * width // hd,
        ),
    )(routes, kv_local, down, tokens, acts, q, g, o, gates, gate_up)


def body(
    grad_out,
    routes,
    gate_probs,
    saved_pre,
    down_weight,
    gate_up_weight,
    queries,
    keys_values,
    attn_grad,
    attn_out,
):
    experts = lax.axis_size("exp")
    contexts = lax.axis_size("ctx")
    tok_rows = grad_out.shape[1]
    filled = saved_pre.shape[2] // experts
    capacity = -(-filled // 16) * 16
    hidden = down_weight.shape[1]
    chips = contexts // 2

    pre_acts = saved_pre[0, 0]
    if capacity != filled:
        pre_acts = pre_acts.reshape(experts, filled, 2 * hidden)
        pre_acts = jnp.pad(pre_acts, ((0, 0), (0, capacity - filled), (0, 0)))
        pre_acts = pre_acts.reshape(experts * capacity, 2 * hidden)
    query_grad, kv_grad, moe_input_grad, token_prob = layer_backward(
        routes.reshape(1, tok_rows),
        keys_values[0],
        down_weight[0],
        grad_out[0],
        pre_acts,
        queries[0],
        attn_grad[0],
        attn_out[0],
        gate_probs[0],
        gate_up_weight[0],
        chips,
        experts,
    )
    prob_grad = token_prob[:, :1][None]
    return (moe_input_grad[None], prob_grad, query_grad[None], kv_grad[None])


def solution(mesh):
    tok = P("exp", "ctx", None)
    placed = (
        tok,
        tok,
        tok,
        P("ctx", "exp", None, None),
        P("exp", None, "ctx"),
        tok,
        tok,
        tok,
        tok,
        tok,
    )
    return jax.shard_map(
        body,
        mesh=mesh,
        in_specs=placed,
        out_specs=(tok, tok, tok, tok),
        check_vma=False,
    )
```
